32 devices in a mesh: ctx: 4 (over y, x), exp: 8 (over z, core).
Axes of the slice: x: 2, y: 2, z: 4, core: 2. Of those that a mesh axis runs over, the one named last changes fastest.
Arguments:
- tokens: bfloat16 [8, 2048, 1024], P('exp', 'ctx'), may hold values from -6 to 6
- attn_gain: float32 [1024], replicated, may hold values from 0.25 to 1.75
- query_weight: bfloat16 [1024, 1024], replicated, may hold values from -0.75 to 0.75
- key_weight: bfloat16 [1024, 512], replicated, may hold values from -0.75 to 0.75
- value_weight: bfloat16 [1024, 512], replicated, may hold values from -0.1875 to 0.1875
- output_weight: bfloat16 [1024, 1024], replicated, may hold values from -1.5 to 1.5
- moe_gain: float32 [1024], replicated, may hold values from 0.25 to 1.75
- w_router: bfloat16 [1024, 32], replicated, may hold values from -0.09375 to 0.09375
- routes: int32 [8, 2048, 8], P('exp', 'ctx'), may hold values from 0 to 31, all different within a row; in each aligned block of 512 rows (0 to 511, 512 to 1023, ..., all dimensions but the last counted through in order) at most 192 rows name the same one
- w_gate: bfloat16 [32, 1024, 512], P('exp'), may hold values from -0.1875 to 0.1875
- w_up: bfloat16 [32, 1024, 512], P('exp'), may hold values from -0.1875 to 0.1875
- w_down: bfloat16 [32, 512, 1024], P('exp'), may hold values from -1.5 to 1.5
- cotangent: bfloat16 [8, 2048, 1024], P('exp', 'ctx'), may hold values from -6 to 6
Outputs:
- layer_out: bfloat16 [8, 2048, 1024], P('exp', 'ctx')
- grad_tokens: float32 [8, 2048, 1024], P('exp', 'ctx')
- grad_attn_gain: float32 [1024], replicated
- grad_query: float32 [1024, 1024], replicated
- grad_key: float32 [1024, 512], replicated
- grad_value: float32 [1024, 512], replicated
- grad_out: float32 [1024, 1024], replicated
- grad_moe_gain: float32 [1024], replicated
- grad_router: float32 [1024, 32], replicated
- grad_gate: float32 [32, 1024, 512], P('exp')
- grad_up: float32 [32, 1024, 512], P('exp')
- grad_down: float32 [32, 512, 1024], P('exp')
The draws below stay inside these ranges and needn't reach their ends.
Inputs may be any that keep to these rules, and one draw needn't show every extreme that they name: `routes`: each token names 8 different experts; among the 512 rows of one device (consecutive positions of one sequence) no expert is named by more than 192 rows, a bound that some block reaches.
All inputs are finite; a program needn't handle non-finite values.
Results may differ from the reference program's by a relative error of at most 0.03.
Values may be sent and summed in bfloat16 or wider, within the bound.
No kernel may reach another device: no remote copies, remote signals or barrier semaphores. Data moves between devices by JAX's collectives and lax.ppermute only.
A program may use at most 256 MiB of HBM per device.

```python
import math
import jax
import jax.numpy as jnp
import numpy as np
from jax import lax

D = 1024
HEADS = 16
KV_HEADS = 8
HEAD_DIM = 64
EXPERTS = 32
FF = 512
TOPK = 8
TOK_DEV = 512
CAP = 192
SEQ_LEN = 2048
SEQS = 8


def steps_of(key, shape, cuts, smallest, high):
    loudness = 1.0
    for axis_at, blocks in cuts:
        heights = jax.random.uniform(jax.random.fold_in(jax.random.fold_in(key, 6), axis_at), (blocks,), jnp.float32, smallest / len(cuts), high / len(cuts))
        loudness = loudness * jnp.repeat(jnp.exp(heights), shape[axis_at] // blocks).reshape((-1,) + (1,) * (len(shape) - 1 - axis_at))
    return loudness


def shared_out(stream_key, own, number, rows, count, top, limit, skew):
    ranking = jax.random.permutation(stream_key, count)
    heavy_load, ordinary = load_shares(count, rows * top, limit, skew, True), load_shares(count, rows * top, limit, skew, False)
    places = jnp.arange(count)

    def named(tallies, rotation):
        used = int((tallies > 0).sum())
        fixed = max(1, used // 4)
        shifted = fixed + (places - fixed + rotation * (used - fixed)) % max(1, count - fixed)
        return jnp.zeros((count,), jnp.int32).at[ranking[jnp.where(places < fixed, places, shifted)]].set(jnp.asarray(tallies, jnp.int32))

    tallies = jnp.where(number % 4 == 0, named(heavy_load, number // 4), named(ordinary, number - number // 4 - 1))
    mixed = jax.random.permutation(jax.random.fold_in(own, 3), count)
    donor, receiver = mixed[0:count // 2 * 2:2], mixed[1:count // 2 * 2:2]
    slack = jnp.minimum(tallies[donor] - 1, limit - tallies[receiver]) // 2
    slack = jnp.where((donor == ranking[0]) | (receiver == ranking[0]) | (tallies[receiver] == 0), 0, jnp.maximum(slack, 0))
    shifted = jax.random.randint(jax.random.fold_in(own, 4), (count // 2,), 0, 1 << 20) % (slack + 1)
    tallies = tallies.at[donor].add(-shifted).at[receiver].add(shifted)
    members = jnp.searchsorted(jnp.cumsum(tallies), jnp.arange(rows * top), side="right").astype(jnp.int32)
    listing = members.reshape(top, rows).T
    listing = listing[jax.random.permutation(jax.random.fold_in(own, 1), rows)]
    rotation = jax.random.randint(jax.random.fold_in(own, 2), (rows, 1), 0, top)
    return jnp.take_along_axis(listing, (jnp.arange(top)[None, :] + rotation) % top, axis=1)


def load_shares(amount, total, most, skew, full):
    weights = [(1 << 20) // math.isqrt(grade ** skew) + 1 for grade in range(1, amount + 1)]
    largest = most if full else min(most, max(-(-total // amount), total * weights[0] // sum(weights)))
    least = 1 if total - largest >= amount - 1 else 0
    counts, surplus = [largest] + [least] * (amount - 1), total - largest - least * (amount - 1)
    while surplus > 0:
        movable = [i for i in range(1, amount) if counts[i] < largest] or [i for i in range(1, amount) if counts[i] < most]
        whole, budget = sum([weights[i] for i in movable]), surplus
        for i in movable:
            more = min(most - counts[i], max(1, budget * weights[i] // whole), surplus)
            counts[i] = counts[i] + more
            surplus = surplus - more
    return np.array(counts)


def normal_values(key, extent, width, bound, split=(), kind=jnp.bfloat16):
    values = jax.random.normal(key, extent, jnp.float32) * width
    if len(split) > 0:
        values = steps_of(key, extent, split, -0.22, 0.18) * values
    return jnp.clip(values, min=-bound, max=bound).astype(kind)


def setup_inputs(seed: int = 0) -> dict:
    key_of = jax.random.split(jax.random.key(seed), 14)
    tokens = normal_values(key_of[0], (SEQS, SEQ_LEN, D), 1.0, 6.0, ((0, 8), (1, 4)))
    attn_gain = jnp.clip(1.0 + 0.15 * jax.random.normal(key_of[1], (D,), jnp.float32), 0.25, 1.75)
    query_weight = normal_values(key_of[2], (D, HEADS * HEAD_DIM), (D // 16) ** -0.5, 0.75)
    key_weight = normal_values(key_of[3], (D, KV_HEADS * HEAD_DIM), (D // 16) ** -0.5, 0.75)
    value_weight = normal_values(key_of[4], (D, KV_HEADS * HEAD_DIM), D ** -0.5, 0.1875)
    output_weight = normal_values(key_of[5], (HEADS * HEAD_DIM, D), (D // 64) ** -0.5, 1.5)
    moe_gain = jnp.clip(1.0 + 0.15 * jax.random.normal(key_of[6], (D,), jnp.float32), 0.25, 1.75)
    w_router = normal_values(key_of[7], (D, EXPERTS), (4 * D) ** -0.5, 0.09375)
    routes_keys = jax.random.split(jax.random.fold_in(key_of[8], 1), SEQS * SEQ_LEN // TOK_DEV)
    routes_turns = jax.random.permutation(jax.random.fold_in(key_of[8], 3), SEQS * SEQ_LEN // TOK_DEV)
    routes = jax.vmap(lambda own, number: shared_out(jax.random.fold_in(key_of[8], 2), own, number, TOK_DEV, EXPERTS, TOPK, CAP, 1))(routes_keys, routes_turns).reshape((SEQS, SEQ_LEN, TOPK))
    w_gate = normal_values(key_of[9], (EXPERTS, D, FF), D ** -0.5, 0.1875, ((0, 8),))
    w_up = normal_values(key_of[10], (EXPERTS, D, FF), D ** -0.5, 0.1875, ((0, 8),))
    w_down = normal_values(key_of[11], (EXPERTS, FF, D), (FF // 32) ** -0.5, 1.5, ((0, 8),))
    cotangent = normal_values(key_of[12], (SEQS, SEQ_LEN, D), 1.0, 6.0, ((0, 8), (1, 4)))
    return {"tokens": tokens, "attn_gain": attn_gain, "query_weight": query_weight, "key_weight": key_weight, "value_weight": value_weight, "output_weight": output_weight, "moe_gain": moe_gain, "w_router": w_router, "routes": routes, "w_gate": w_gate, "w_up": w_up, "w_down": w_down, "cotangent": cotangent}


@jax.custom_vjp
def low(v):
    return lax.optimization_barrier(v.astype(jnp.bfloat16)).astype(jnp.float32)

@jax.custom_vjp
def lower_backward(v):
    return v

def low_keep(v):
    return (low(v), None)

def low_pass(kept, grad):
    return (grad,)

def back_keep(v):
    return (v, None)

def back_low(kept, grad):
    return (low(grad),)
low.defvjp(low_keep, low_pass)
lower_backward.defvjp(back_keep, back_low)
FULL_PRECISION = lax.Precision.HIGHEST
EPSILON = 1e-06
SCALE = 0.015625
THETA = 10000.0
NEG = -1e+30

def rms_scaled(values, gain):
    factor = lax.rsqrt(lax.optimization_barrier(jnp.mean(values * values, axis=-1, keepdims=True)) + EPSILON)
    return values * factor * gain

def rotate(values, positions):
    half_size = values.shape[-1] // 2
    inverse = THETA ** (-jnp.arange(half_size, dtype=jnp.float32) * 2.0 / values.shape[-1])
    angles = positions.astype(jnp.float32)[:, None] * inverse[None, :]
    cosine_table = jnp.concatenate([jnp.cos(angles), jnp.cos(angles)], -1)[:, None, :]
    sine_table = jnp.concatenate([jnp.sin(angles), jnp.sin(angles)], -1)[:, None, :]
    turned = jnp.concatenate([-values[..., half_size:], values[..., :half_size]], -1)
    return values * cosine_table + turned * sine_table

def attend(queries, key_rows, value_rows):
    query_block = min(512, SEQ_LEN)
    block_total = SEQ_LEN // query_block
    grouped = queries.reshape(block_total, query_block, KV_HEADS, HEADS // KV_HEADS, HEAD_DIM)
    places = jnp.arange(SEQ_LEN, dtype=jnp.int32)

    def one_block(item):
        block_queries, block_index = item
        scores = jnp.einsum('qkgd,nkd->qkgn', block_queries, key_rows, precision=FULL_PRECISION) * SCALE
        scores = lower_backward(scores)
        rows_here = block_index * query_block + jnp.arange(query_block, dtype=jnp.int32)
        allowed = (places[None, :] <= rows_here[:, None])[:, None, None, :]
        probs = low(jax.nn.softmax(jnp.where(allowed, scores, NEG), axis=-1))
        return jnp.einsum('qkgn,nkd->qkgd', probs, value_rows, precision=FULL_PRECISION)
    result = lax.map(jax.checkpoint(one_block), (grouped, jnp.arange(block_total, dtype=jnp.int32)))
    return result.reshape(SEQ_LEN, HEADS * HEAD_DIM)

def experts_ffn(normed, route_rows, w_router, w_gate, w_up, w_down):
    row_total = normed.shape[0]
    block_total = row_total // TOK_DEV
    logits = lower_backward(jnp.dot(normed, w_router, precision=FULL_PRECISION))
    chosen = jnp.take_along_axis(logits, route_rows, axis=1)
    gate_weights = jax.nn.softmax(chosen, axis=-1)
    one_hot = (route_rows[..., None] == jnp.arange(EXPERTS, dtype=jnp.int32)).astype(jnp.int32)
    one_hot = one_hot.reshape(block_total, TOK_DEV * TOPK, EXPERTS)
    slot_index = lax.optimization_barrier(jnp.sum((jnp.cumsum(one_hot, axis=1, dtype=jnp.int32) - 1) * one_hot, axis=-1, dtype=jnp.int32))
    slot_index = slot_index.reshape(row_total, TOPK)
    block_id = (jnp.arange(row_total, dtype=jnp.int32) // TOK_DEV)[:, None]
    targets = (route_rows * (block_total * CAP) + block_id * CAP + slot_index).reshape(-1).astype(jnp.int32)
    token_index = jnp.repeat(jnp.arange(row_total, dtype=jnp.int32), TOPK)
    buffer = jnp.zeros((EXPERTS * block_total * CAP, D), normed.dtype).at[targets].set(normed[token_index])
    buffer = lower_backward(buffer).reshape(EXPERTS, block_total * CAP, D)
    gate_lin = lower_backward(jnp.einsum('emd,edf->emf', buffer, w_gate, precision=FULL_PRECISION))
    up_lin = lower_backward(jnp.einsum('emd,edf->emf', buffer, w_up, precision=FULL_PRECISION))
    hidden = low(jax.nn.silu(gate_lin) * up_lin)
    produced = low(lower_backward(jnp.einsum('emf,efd->emd', hidden, w_down, precision=FULL_PRECISION)))
    picked = produced.reshape(-1, D)[targets].reshape(row_total, TOPK, D)
    return lax.optimization_barrier(jnp.sum(gate_weights[..., None] * picked, axis=1))

def layer(layer_inputs, route_rows, weights):
    attn_gain, query_weight, key_weight, value_weight, output_weight, moe_gain, w_router, w_gate, w_up, w_down = weights
    group = layer_inputs.shape[0]
    places = jnp.arange(SEQ_LEN, dtype=jnp.int32)
    first_normalized = low(rms_scaled(layer_inputs, attn_gain))
    query_linear = lower_backward(jnp.einsum('orn,nv->orv', first_normalized, query_weight, precision=FULL_PRECISION))
    key_linear = lower_backward(jnp.einsum('orn,nv->orv', first_normalized, key_weight, precision=FULL_PRECISION))
    value_linear = lower_backward(jnp.einsum('orn,nv->orv', first_normalized, value_weight, precision=FULL_PRECISION))
    queries = low(rotate(query_linear.reshape(group, SEQ_LEN, HEADS, HEAD_DIM), places))
    queries = queries.reshape(group, SEQ_LEN, KV_HEADS, HEADS // KV_HEADS, HEAD_DIM)
    key_rows = low(rotate(key_linear.reshape(group, SEQ_LEN, KV_HEADS, HEAD_DIM), places))
    value_rows = low(value_linear).reshape(group, SEQ_LEN, KV_HEADS, HEAD_DIM)
    attention_result = lax.map(lambda item: attend(item[0], item[1], item[2]), (queries, key_rows, value_rows))
    attention_result = low(lower_backward(attention_result))
    residual_stream = layer_inputs + lower_backward(jnp.einsum('amu,uc->amc', attention_result, output_weight, precision=FULL_PRECISION))
    normed_two = low(rms_scaled(residual_stream, moe_gain))
    mixture = experts_ffn(normed_two.reshape(group * SEQ_LEN, D), route_rows.reshape(group * SEQ_LEN, TOPK), w_router, w_gate, w_up, w_down)
    return residual_stream + mixture.reshape(group, SEQ_LEN, D)

def reference(tokens, attn_gain, query_weight, key_weight, value_weight, output_weight, moe_gain, w_router, routes, w_gate, w_up, w_down, cotangent):
    group = math.gcd(SEQS, max(1, 2048 // SEQ_LEN))
    grouped_routes = routes.reshape(SEQS // group, group, SEQ_LEN, TOPK)

    def forward(layer_inputs, *weights):
        grouped = layer_inputs.reshape(SEQS // group, group, SEQ_LEN, D)

        def step(carried, item):
            return (carried, layer(item[0], item[1], weights))
        _, outputs = lax.scan(jax.checkpoint(step), jnp.zeros((), jnp.float32), (grouped, grouped_routes))
        return outputs.reshape(SEQS, SEQ_LEN, D)
    weights = tuple((w.astype(jnp.float32) for w in (attn_gain, query_weight, key_weight, value_weight, output_weight, moe_gain, w_router, w_gate, w_up, w_down)))
    output, pull = jax.vjp(forward, tokens.astype(jnp.float32), *weights)
    grads = pull(cotangent.astype(jnp.float32))
    return (output.astype(jnp.bfloat16), grads[0], grads[1], grads[2], grads[3], grads[4], grads[5], grads[6], grads[7], grads[8], grads[9], grads[10])
```

```python
import functools

import jax
import jax.numpy as jnp
from jax import lax
from jax.experimental import pallas as pl
from jax.experimental.pallas import tpu as pltpu
from jax.sharding import PartitionSpec as P

HEAD_DIM = 64
CAP = 192


SCALE = 0.015625
THETA = 10000.0
EPSILON = 1e-06
NEG = -1e30

F32 = jnp.float32
BF16 = jnp.bfloat16
NN = (((1,), (0,)), ((), ()))
NT = (((1,), (1,)), ((), ()))
TN = (((0,), (0,)), ((), ()))


def mm(left, right, dims=NN):
    return lax.dot_general(left, right, dims, preferred_element_type=F32)


def normalize(values):
    factor = lax.rsqrt(jnp.mean(values * values, axis=-1, keepdims=True) + EPSILON)
    return (values * factor, factor)


def norm_back(grad_scaled, scaled, factor):
    return factor * (grad_scaled - scaled * jnp.mean(grad_scaled * scaled, axis=-1, keepdims=True))


def rotate_columns(values, cosine, sine, direction):
    half = HEAD_DIM // 2
    split = values.reshape(-1, 2, half, values.shape[-1])
    first, second = split[:, 0], split[:, 1]
    turned = direction * sine
    return jnp.stack(
        [first * cosine - second * turned, second * cosine + first * turned], axis=1
    ).reshape(values.shape)


def head_columns(block, which):
    low = 2 * HEAD_DIM * which
    pair = jnp.concatenate(
        [block[low : low + HEAD_DIM], block[low + HEAD_DIM : low + 2 * HEAD_DIM]], axis=1
    )
    empty = jnp.zeros_like(pair)
    return jnp.concatenate([pair, empty] if which == 0 else [empty, pair], axis=0)


def causal(rows):
    keys = lax.broadcasted_iota(jnp.int32, (rows, rows), 0)
    places = lax.broadcasted_iota(jnp.int32, (rows, rows), 1)
    one = keys <= places
    return jnp.concatenate([one, one], axis=1)


def attend_kernel(own_ref, q_ref, k_ref, v_ref, wide_ref, low_ref, log_ref):
    rows = q_ref.shape[1]
    own = own_ref[0]
    columns = [head_columns(q_ref[...], which) for which in range(2)]

    def visit(block, carried, masked):
        at = pl.ds(pl.multiple_of(block * rows, rows), rows)
        keys = k_ref[at, :]
        values = v_ref[at, :].T
        result = []
        for which in range(2):
            running, mass, total = carried[which]
            scores = mm(keys, columns[which])
            if masked:
                scores = jnp.where(causal(rows), scores, NEG)
            newest = jnp.maximum(running, jnp.max(scores, axis=0, keepdims=True))
            weights = jnp.exp(scores - newest)
            rescale = jnp.exp(running - newest)
            mass = mass * rescale + jnp.sum(weights, axis=0, keepdims=True)
            mine = values[which * HEAD_DIM : (which + 1) * HEAD_DIM]
            total = total * rescale + mm(mine, weights.astype(BF16))
            result.append((newest, mass, total))
        return tuple(result)

    initial = tuple(
        (
            jnp.full((1, 2 * rows), NEG, F32),
            jnp.zeros((1, 2 * rows), F32),
            jnp.zeros((HEAD_DIM, 2 * rows), F32),
        )
        for _ in range(2)
    )
    carried = visit(own, initial, True)
    carried = lax.fori_loop(0, own, lambda block, inner: visit(block, inner, False), carried)
    for which in range(2):
        running, mass, total = carried[which]
        result = total / mass
        logs = running + jnp.log(mass)
        for group in range(2):
            head = 2 * which + group
            part = slice(group * rows, (group + 1) * rows)
            wide_ref[head * HEAD_DIM : (head + 1) * HEAD_DIM, :] = result[:, part]
            log_ref[0, head : head + 1, :] = logs[:, part]
    low_ref[...] = wide_ref[...].T.astype(BF16)


def attend_back_kernel(
    own_ref, q_ref, k_ref, v_ref, grad_ref, wide_ref, log_ref, dq_ref, dk_ref, dv_ref, sum_ref
):
    rows = q_ref.shape[1]
    own = own_ref[0]
    columns = [head_columns(q_ref[...], which) for which in range(2)]
    grads = [head_columns(grad_ref[...], which) for which in range(2)]
    offsets, logs = [], []
    for which in range(2):
        pieces = []
        for group in range(2):
            part = slice((2 * which + group) * HEAD_DIM, (2 * which + group + 1) * HEAD_DIM)
            pieces.append(
                jnp.sum(grad_ref[part, :].astype(F32) * wide_ref[part, :], axis=0, keepdims=True)
            )
        offsets.append(jnp.concatenate(pieces, axis=1))
        logs.append(
            jnp.concatenate(
                [log_ref[0, 2 * which : 2 * which + 1, :], log_ref[0, 2 * which + 1 : 2 * which + 2, :]],
                axis=1,
            )
        )
    sum_ref[...] = jnp.zeros_like(sum_ref)
    dk_ref[...] = jnp.zeros_like(dk_ref)
    dv_ref[...] = jnp.zeros_like(dv_ref)

    def visit(block, masked):
        at = pl.ds(pl.multiple_of(block * rows, rows), rows)
        keys = k_ref[at, :]
        values = v_ref[at, :]
        turned = keys.T
        key_sum, value_sum = None, None
        for which in range(2):
            soft = jnp.exp(mm(keys, columns[which]) - logs[which])
            if masked:
                soft = jnp.where(causal(rows), soft, 0.0)
            prob_grad = mm(values, grads[which])
            score_grad = (soft * (prob_grad - offsets[which])).astype(BF16)
            value_part = mm(soft.astype(BF16), grads[which], NT)
            key_part = mm(score_grad, columns[which], NT)
            key_sum = key_part if key_sum is None else key_sum + key_part
            value_sum = value_part if value_sum is None else value_sum + value_part
            mine = slice(which * HEAD_DIM, (which + 1) * HEAD_DIM)
            sum_ref[mine, :] += mm(turned[mine], score_grad)
        dk_ref[at, :] = key_sum.astype(BF16)
        dv_ref[at, :] = value_sum.astype(BF16)

    visit(own, True)
    lax.fori_loop(0, own, lambda block, inner: (visit(block, False), inner)[1], 0)
    for which in range(2):
        for group in range(2):
            head = 2 * which + group
            dq_ref[head * HEAD_DIM : (head + 1) * HEAD_DIM, :] = (
                sum_ref[
                    which * HEAD_DIM : (which + 1) * HEAD_DIM, group * rows : (group + 1) * rows
                ]
                * SCALE
            )


def attend(own, queries, keys, values):
    width, rows = queries.shape
    length, kv_width = keys.shape
    pairs = kv_width // (2 * HEAD_DIM)
    step = width // pairs
    heads = step // HEAD_DIM
    return pl.pallas_call(
        attend_kernel,
        grid=(pairs,),
        in_specs=[
            pl.BlockSpec(memory_space=pltpu.SMEM),
            pl.BlockSpec((step, rows), lambda p: (p, 0)),
            pl.BlockSpec((length, 2 * HEAD_DIM), lambda p: (0, p)),
            pl.BlockSpec((length, 2 * HEAD_DIM), lambda p: (0, p)),
        ],
        out_specs=[
            pl.BlockSpec((step, rows), lambda p: (p, 0)),
            pl.BlockSpec((rows, step), lambda p: (0, p)),
            pl.BlockSpec((1, heads, rows), lambda p: (p, 0, 0)),
        ],
        out_shape=[
            jax.ShapeDtypeStruct((width, rows), F32),
            jax.ShapeDtypeStruct((rows, width), BF16),
            jax.ShapeDtypeStruct((pairs, heads, rows), F32),
        ],
        compiler_params=pltpu.CompilerParams(vmem_limit_bytes=48 * 1024 * 1024),
        name="attend",
    )(own, queries, keys, values)


def attend_back(own, queries, keys, values, grads, wide, logs):
    width, rows = queries.shape
    length, kv_width = keys.shape
    pairs = kv_width // (2 * HEAD_DIM)
    step = width // pairs
    heads = step // HEAD_DIM
    columns = pl.BlockSpec((step, rows), lambda p: (p, 0))
    whole = pl.BlockSpec((length, 2 * HEAD_DIM), lambda p: (0, p))
    return pl.pallas_call(
        attend_back_kernel,
        grid=(pairs,),
        in_specs=[
            pl.BlockSpec(memory_space=pltpu.SMEM),
            columns,
            whole,
            whole,
            columns,
            columns,
            pl.BlockSpec((1, heads, rows), lambda p: (p, 0, 0)),
        ],
        out_specs=[columns, whole, whole],
        out_shape=[
            jax.ShapeDtypeStruct((width, rows), F32),
            jax.ShapeDtypeStruct((length, kv_width), BF16),
            jax.ShapeDtypeStruct((length, kv_width), BF16),
        ],
        scratch_shapes=[pltpu.VMEM((2 * HEAD_DIM, 2 * rows), F32)],
        compiler_params=pltpu.CompilerParams(vmem_limit_bytes=48 * 1024 * 1024),
        name="attend_back",
    )(own, queries, keys, values, grads, wide, logs)


def experts_kernel(blocks, owned, first, *refs):
    if first:
        x_ref, c_ref, rank_ref, mask_ref, router_ref, gate_ref, up_ref, down_ref = refs[:8]
        olds = (None, None, None)
        rest = refs[8:]
    else:
        x_ref, c_ref, rank_ref, mask_ref, router_ref, gate_ref, up_ref, down_ref = refs[:8]
        olds = refs[8:11]
        rest = refs[11:]
    (
        y_ref,
        dx_ref,
        dgate_ref,
        dup_ref,
        ddown_ref,
        chosen_ref,
        rows_x,
        rows_c,
        rows_w,
    ) = rest
    step = pl.program_id(0)
    tokens = x_ref.shape[1]

    def hot(block, expert):
        slots = lax.broadcasted_iota(jnp.int32, (CAP, tokens), 0)
        return slots == rank_ref[block, pl.ds(expert, 1), :]

    def places(block):
        return jnp.concatenate(
            [hot(block, e).astype(F32).astype(BF16) for e in range(owned)], axis=0
        )

    @pl.when(step < blocks)
    def gather():
        block = step
        at = pl.ds(pl.multiple_of(block * CAP, CAP), CAP)
        select = places(block)
        picked = mm(select, x_ref[0]).astype(BF16)
        upstream = mm(select, c_ref[0]).astype(BF16)
        logits = mm(picked, router_ref[...])
        named = mm(select, mask_ref[block]) > 0.5
        masked = jnp.where(named, logits, NEG)
        grown = jnp.where(
            named, jnp.exp(masked - jnp.max(masked, axis=1, keepdims=True)), 0.0
        )
        mass = jnp.sum(grown, axis=1, keepdims=True)
        weights = grown / jnp.where(mass > 0.0, mass, 1.0)
        for e in range(owned):
            part = slice(e * CAP, (e + 1) * CAP)
            rows_x[e, at, :] = picked[part]
            rows_c[e, at, :] = upstream[part]
            rows_w[e, at, :] = weights[part, e : e + 1]

    @pl.when((step >= blocks) & (step < blocks + owned))
    def multiply():
        e = step - blocks
        x = rows_x[e]
        c = rows_c[e]
        weight = rows_w[e]
        gate = mm(x, gate_ref[0])
        up = mm(x, up_ref[0])
        back = mm(c, down_ref[0], NT)
        sigmoid = 1.0 / (1.0 + jnp.exp(-gate))
        activated = gate * sigmoid
        hidden = activated * up
        scored = jnp.sum(hidden * back, axis=1, keepdims=True)
        for block in range(blocks):
            part = scored[block * CAP : (block + 1) * CAP]
            chosen_ref[0, block : block + 1, :] = jnp.sum(
                jnp.where(hot(block, e), part, 0.0), axis=0, keepdims=True
            )
        weighted = (hidden * weight).astype(BF16)
        back = back * weight
        gate_back = (back * up * sigmoid * (1.0 + gate * (1.0 - sigmoid))).astype(BF16)
        up_back = (back * activated).astype(BF16)
        turned = x.T
        grads = (mm(turned, gate_back), mm(turned, up_back), mm(weighted.T, c))
        for out_ref, old_ref, grad in zip((dgate_ref, dup_ref, ddown_ref), olds, grads):
            if old_ref is not None:
                grad = grad + old_ref[0].astype(F32)
            out_ref[0] = grad.astype(BF16)
        rows_c[e] = mm(weighted, down_ref[0]).astype(BF16)
        rows_x[e] = (mm(gate_back, gate_ref[0], NT) + mm(up_back, up_ref[0], NT)).astype(BF16)

    @pl.when(step >= blocks + owned)
    def scatter():
        block = step - blocks - owned
        at = pl.ds(pl.multiple_of(block * CAP, CAP), CAP)
        select = places(block).T
        y_ref[0] = mm(
            select, jnp.concatenate([rows_c[e, at, :] for e in range(owned)], axis=0)
        ).astype(BF16)
        dx_ref[0] = mm(
            select, jnp.concatenate([rows_x[e, at, :] for e in range(owned)], axis=0)
        ).astype(BF16)


def run_experts(x, c, rank, mask, router, w_gate, w_up, w_down, olds):
    blocks, tokens, width = x.shape
    owned, _, hidden = w_gate.shape
    first = olds is None

    def entering(s):
        return (jnp.minimum(s, blocks - 1), 0, 0)

    def expert(s):
        return (jnp.clip(s - blocks, 0, owned - 1), 0, 0)

    def leaving(s):
        return (jnp.clip(s - blocks - owned, 0, blocks - 1), 0, 0)

    def fixed(*shape):
        return pl.BlockSpec(shape, lambda s: (0,) * len(shape))

    grads = [
        pl.BlockSpec((1, width, hidden), expert),
        pl.BlockSpec((1, width, hidden), expert),
        pl.BlockSpec((1, hidden, width), expert),
    ]
    return pl.pallas_call(
        functools.partial(experts_kernel, blocks, owned, first),
        grid=(2 * blocks + owned,),
        in_specs=[
            pl.BlockSpec((1, tokens, width), entering),
            pl.BlockSpec((1, tokens, width), entering),
            fixed(*rank.shape),
            fixed(*mask.shape),
            fixed(*router.shape),
            *grads,
            *([] if first else grads),
        ],
        out_specs=[
            pl.BlockSpec((1, tokens, width), leaving),
            pl.BlockSpec((1, tokens, width), leaving),
            *grads,
            pl.BlockSpec((1, blocks, tokens), expert),
        ],
        out_shape=[
            jax.ShapeDtypeStruct(x.shape, BF16),
            jax.ShapeDtypeStruct(x.shape, BF16),
            jax.ShapeDtypeStruct(w_gate.shape, BF16),
            jax.ShapeDtypeStruct(w_up.shape, BF16),
            jax.ShapeDtypeStruct(w_down.shape, BF16),
            jax.ShapeDtypeStruct((owned, blocks, tokens), F32),
        ],
        scratch_shapes=[
            pltpu.VMEM((owned, blocks * CAP, width), BF16),
            pltpu.VMEM((owned, blocks * CAP, width), BF16),
            pltpu.VMEM((owned, blocks * CAP, 1), F32),
        ],
        compiler_params=pltpu.CompilerParams(vmem_limit_bytes=60 * 1024 * 1024),
        name="experts",
    )(x, c, rank, mask, router, w_gate, w_up, w_down, *([] if first else olds))


def swap(value, bit, peers):
    return lax.ppermute(value, "exp", [(i, i ^ bit) for i in range(peers)])


def gather_blocks(value, peers):
    held = {0: value}
    bit = peers // 2
    while bit >= 1:
        for m in list(held):
            held[m | bit] = swap(held[m], bit, peers)
        bit //= 2
    return [held[m] for m in range(peers)]


def reduce_blocks(parts, peers):
    held = dict(enumerate(parts))
    bit = 1
    while bit < peers:
        for m in sorted(held, reverse=True):
            if m & bit:
                arrived = swap(held.pop(m), bit, peers)
                held[m ^ bit] = (
                    held[m ^ bit].astype(F32) + arrived.astype(F32)
                ).astype(BF16)
        bit *= 2
    return held[0]


def per_device(
    tokens,
    attn_gain,
    query_weight,
    key_weight,
    value_weight,
    output_weight,
    moe_gain,
    w_router,
    routes,
    w_gate,
    w_up,
    w_down,
    cotangent,
):
    tok_rows = tokens.shape[1]
    model_width = tokens.shape[2]
    experts = w_router.shape[1]
    owned = w_gate.shape[0]
    peers = lax.axis_size("exp")
    here = lax.axis_index("exp")
    own = lax.axis_index("ctx")
    positions = own * tok_rows + jnp.arange(tok_rows, dtype=jnp.int32)
    half = HEAD_DIM // 2
    inverse = THETA ** (-jnp.arange(half, dtype=F32) * 2.0 / HEAD_DIM)
    angles = inverse[:, None] * positions.astype(F32)[None, :]
    cosine, sine = jnp.cos(angles), jnp.sin(angles)

    cot_blocks = gather_blocks(cotangent[0], peers)
    route_blocks = jnp.stack(gather_blocks(routes[0], peers))
    order = jnp.arange(experts, dtype=jnp.int32)
    order = ((order // owned) ^ here) * owned + order % owned
    permutation = (jnp.arange(experts, dtype=jnp.int32)[:, None] == order[None, :]).astype(BF16)
    named = jnp.any(route_blocks[..., None] == order, axis=2)
    mask = named.astype(BF16)
    earlier = jnp.tril(jnp.ones((tok_rows, tok_rows), BF16))
    rank = jnp.einsum(
        "ts,bse->bet", earlier, mask[..., :owned], preferred_element_type=F32
    ).astype(jnp.int32)
    rank = jnp.where(jnp.swapaxes(named[..., :owned], 1, 2), rank - 1, -1)
    router = mm(w_router, permutation).astype(BF16)

    layer_inputs = tokens[0].astype(F32)
    scaled_one, factor_one = normalize(layer_inputs)
    first_normalized = (scaled_one * attn_gain).astype(BF16)
    value_rows = mm(first_normalized, value_weight).astype(BF16)
    key_turned = rotate_columns(
        jnp.einsum("de,td->et", key_weight, first_normalized, preferred_element_type=F32),
        cosine,
        sine,
        1.0,
    ).astype(BF16)
    key_rows = key_turned.T
    queries = (
        rotate_columns(
            jnp.einsum("de,td->et", query_weight, first_normalized, preferred_element_type=F32),
            cosine,
            sine,
            1.0,
        ).astype(BF16)
        * SCALE
    ).astype(BF16)
    keys = lax.all_gather(key_rows, "ctx", axis=0, tiled=True)
    values = lax.all_gather(value_rows, "ctx", axis=0, tiled=True)
    own_index = jnp.full((1,), own, jnp.int32)
    attended_wide, attended_low, logs = attend(own_index, queries, keys, values)
    residual_stream = layer_inputs + mm(attended_low, output_weight)
    scaled_two, factor_two = normalize(residual_stream)
    normed_two = (scaled_two * moe_gain).astype(BF16)

    x_blocks = gather_blocks(normed_two, peers)
    olds = None
    mixed, dx, chosen = [], [], []
    group = min(4, peers)
    for start in range(0, peers, group):
        part = slice(start, start + group)
        y_part, dx_part, *olds, chosen_part = run_experts(
            jnp.stack(x_blocks[part]),
            jnp.stack(cot_blocks[part]),
            rank[part],
            mask[part],
            router,
            w_gate,
            w_up,
            w_down,
            olds,
        )
        mixed += [y_part[i] for i in range(group)]
        dx += [dx_part[i] for i in range(group)]
        chosen += [chosen_part[:, i] for i in range(group)]

    logits = mm(normed_two, router)
    named_here = named[0]
    masked = jnp.where(named_here, logits, NEG)
    grown = jnp.where(named_here, jnp.exp(masked - jnp.max(masked, axis=1, keepdims=True)), 0.0)
    gate_weights = grown / jnp.sum(grown, axis=1, keepdims=True)
    gate_grad = jnp.concatenate(
        [chosen[0]] + [swap(chosen[m], m, peers) for m in range(1, peers)], axis=0
    ).T
    chosen_grad = gate_weights * (
        gate_grad - jnp.sum(gate_weights * gate_grad, axis=-1, keepdims=True)
    )
    logit_grad = mm(chosen_grad.astype(BF16), permutation, NT).astype(BF16)
    router_grad = mm(normed_two, logit_grad, TN)

    upstream = cotangent[0].astype(F32)
    normed_two_grad = mm(logit_grad, w_router, NT) + reduce_blocks(dx, peers).astype(F32)
    output = residual_stream + reduce_blocks(mixed, peers).astype(F32)
    wgate_grad, wup_grad, down_grad = (
        lax.psum(grad, "ctx").astype(F32) for grad in olds
    )
    gain_two_grad = jnp.sum(normed_two_grad * scaled_two, axis=0)
    residual_grad = upstream + norm_back(normed_two_grad * moe_gain, scaled_two, factor_two)
    residual_low = residual_grad.astype(BF16)
    wout_grad = mm(attended_low, residual_low, TN)
    attended_grad = mm(output_weight, residual_low, NT).astype(BF16)

    query_grad, key_sum, value_sum = attend_back(
        own_index, queries, keys, values, attended_grad, attended_wide, logs
    )
    key_grad, value_grad = (
        lax.psum_scatter(part, "ctx", scatter_dimension=0, tiled=True).astype(F32)
        for part in (key_sum, value_sum)
    )
    query_back = rotate_columns(query_grad, cosine, sine, -1.0).astype(BF16)
    key_back = rotate_columns(key_grad.T, cosine, sine, -1.0).astype(BF16)
    value_back = value_grad.astype(BF16)
    wq_grad = jnp.einsum("td,et->de", first_normalized, query_back, preferred_element_type=F32)
    wk_grad = jnp.einsum("td,et->de", first_normalized, key_back, preferred_element_type=F32)
    wv_grad = mm(first_normalized, value_back, TN)
    normed_one_grad = (
        jnp.einsum("et,de->td", query_back, query_weight, preferred_element_type=F32)
        + jnp.einsum("et,de->td", key_back, key_weight, preferred_element_type=F32)
        + mm(value_back, value_weight, NT)
    )
    gain_one_grad = jnp.sum(normed_one_grad * scaled_one, axis=0)
    input_grad = residual_grad + norm_back(normed_one_grad * attn_gain, scaled_one, factor_one)
    early = lax.psum(
        (wout_grad.astype(BF16), router_grad.astype(BF16), gain_two_grad.astype(BF16)),
        ("ctx", "exp"),
    )
    late = lax.psum(
        tuple(g.astype(BF16) for g in (wq_grad, wk_grad, wv_grad, gain_one_grad)),
        ("ctx", "exp"),
    )
    wout_grad, router_grad, gain_two_grad = (g.astype(F32) for g in early)
    wq_grad, wk_grad, wv_grad, gain_one_grad = (g.astype(F32) for g in late)
    return (
        output.astype(BF16)[None],
        input_grad[None],
        gain_one_grad,
        wq_grad,
        wk_grad,
        wv_grad,
        wout_grad,
        gain_two_grad,
        router_grad,
        wgate_grad,
        wup_grad,
        down_grad,
    )


def solution(mesh):
    return jax.shard_map(
        per_device,
        mesh=mesh,
        in_specs=(
            P("exp", "ctx", None),
            P(),
            P(),
            P(),
            P(),
            P(),
            P(),
            P(),
            P("exp", "ctx", None),
            P("exp", None, None),
            P("exp", None, None),
            P("exp", None, None),
            P("exp", "ctx", None),
        ),
        out_specs=(
            P("exp", "ctx", None),
            P("exp", "ctx", None),
            P(),
            P(),
            P(),
            P(),
            P(),
            P(),
            P(),
            P("exp", None, None),
            P("exp", None, None),
            P("exp", None, None),
        ),
        check_vma=False,
    )
```

```python
import functools

import jax
import jax.numpy as jnp
from jax import lax
from jax.experimental import pallas as pl
from jax.experimental.pallas import tpu as pltpu
from jax.sharding import PartitionSpec as P

HEAD_DIM = 64
CAP = 192


SCALE = 0.015625
THETA = 10000.0
EPSILON = 1e-06
NEG = -1e30

F32 = jnp.float32
BF16 = jnp.bfloat16
NN = (((1,), (0,)), ((), ()))
NT = (((1,), (1,)), ((), ()))
TN = (((0,), (0,)), ((), ()))


def mm(left, right, dims=NN):
    return lax.dot_general(left, right, dims, preferred_element_type=F32)


def normalize(values):
    factor = lax.rsqrt(jnp.mean(values * values, axis=-1, keepdims=True) + EPSILON)
    return (values * factor, factor)


def norm_back(grad_scaled, scaled, factor):
    return factor * (grad_scaled - scaled * jnp.mean(grad_scaled * scaled, axis=-1, keepdims=True))


def rotate_columns(values, cosine, sine, direction):
    half = HEAD_DIM // 2
    split = values.reshape(-1, 2, half, values.shape[-1])
    first, second = split[:, 0], split[:, 1]
    turned = direction * sine
    return jnp.stack(
        [first * cosine - second * turned, second * cosine + first * turned], axis=1
    ).reshape(values.shape)


def head_columns(block, which):
    low = 2 * HEAD_DIM * which
    pair = jnp.concatenate(
        [block[low : low + HEAD_DIM], block[low + HEAD_DIM : low + 2 * HEAD_DIM]], axis=1
    )
    empty = jnp.zeros_like(pair)
    return jnp.concatenate([pair, empty] if which == 0 else [empty, pair], axis=0)


def causal(rows):
    keys = lax.broadcasted_iota(jnp.int32, (rows, rows), 0)
    places = lax.broadcasted_iota(jnp.int32, (rows, rows), 1)
    one = keys <= places
    return jnp.concatenate([one, one], axis=1)


def attend_kernel(peers, own_ref, q_ref, *refs):
    k_refs, v_refs = refs[:peers], refs[peers : 2 * peers]
    wide_ref, low_ref, log_ref, running_ref, mass_ref, total_ref = refs[2 * peers :]
    rows = q_ref.shape[1]
    own = own_ref[0]
    columns = [head_columns(q_ref[...], which) for which in range(2)]

    def visit(m):
        keys = k_refs[m][...]
        values = v_refs[m][...].T
        for which in range(2):
            scores = mm(keys, columns[which])
            if m == 0:
                scores = jnp.where(causal(rows), scores, NEG)
            newest = jnp.max(scores, axis=0, keepdims=True)
            if m > 0:
                newest = jnp.maximum(running_ref[which], newest)
            weights = jnp.exp(scores - newest)
            mass = jnp.sum(weights, axis=0, keepdims=True)
            mine = values[which * HEAD_DIM : (which + 1) * HEAD_DIM]
            total = mm(mine, weights.astype(BF16))
            if m > 0:
                rescale = jnp.exp(running_ref[which] - newest)
                mass = mass + mass_ref[which] * rescale
                total = total + total_ref[which] * rescale
            running_ref[which] = newest
            mass_ref[which] = mass
            total_ref[which] = total

    visit(0)
    for m in range(1, peers):
        pl.when((own ^ m) < own)(functools.partial(visit, m))
    for which in range(2):
        result = total_ref[which] / mass_ref[which]
        logs = running_ref[which] + jnp.log(mass_ref[which])
        for group in range(2):
            head = 2 * which + group
            part = slice(group * rows, (group + 1) * rows)
            wide_ref[head * HEAD_DIM : (head + 1) * HEAD_DIM, :] = result[:, part]
            log_ref[0, head : head + 1, :] = logs[:, part]
    low_ref[...] = wide_ref[...].T.astype(BF16)


def attend_back_kernel(peers, own_ref, q_ref, grad_ref, wide_ref, log_ref, cos_ref, sin_ref, *refs):
    k_refs, v_refs = refs[:peers], refs[peers : 2 * peers]
    dq_ref = refs[2 * peers]
    dk_refs = refs[2 * peers + 1 : 3 * peers + 1]
    dv_refs = refs[3 * peers + 1 : 4 * peers + 1]
    sum_ref = refs[4 * peers + 1]
    rows = q_ref.shape[1]
    own = own_ref[0]
    columns = [head_columns(q_ref[...], which) for which in range(2)]
    grads = [head_columns(grad_ref[...], which) for which in range(2)]
    offsets, logs = [], []
    for which in range(2):
        pieces = []
        for group in range(2):
            part = slice((2 * which + group) * HEAD_DIM, (2 * which + group + 1) * HEAD_DIM)
            pieces.append(
                jnp.sum(grad_ref[part, :].astype(F32) * wide_ref[part, :], axis=0, keepdims=True)
            )
        offsets.append(jnp.concatenate(pieces, axis=1))
        low = 2 * which
        logs.append(
            jnp.concatenate([log_ref[0, low : low + 1, :], log_ref[0, low + 1 : low + 2, :]], axis=1)
        )

    def visit(m):
        keys = k_refs[m][...]
        values = v_refs[m][...]
        turned = keys.T
        key_sum, value_sum = None, None
        for which in range(2):
            soft = jnp.exp(mm(keys, columns[which]) - logs[which])
            if m == 0:
                soft = jnp.where(causal(rows), soft, 0.0)
            prob_grad = mm(values, grads[which])
            score_grad = (soft * (prob_grad - offsets[which])).astype(BF16)
            value_part = mm(soft.astype(BF16), grads[which], NT)
            key_part = mm(score_grad, columns[which], NT)
            key_sum = key_part if key_sum is None else key_sum + key_part
            value_sum = value_part if value_sum is None else value_sum + value_part
            mine = slice(which * HEAD_DIM, (which + 1) * HEAD_DIM)
            part = mm(turned[mine], score_grad)
            sum_ref[mine, :] = part if m == 0 else sum_ref[mine, :] + part
        lanes = lax.broadcasted_iota(jnp.int32, key_sum.shape, 1) % HEAD_DIM
        ahead = pltpu.roll(key_sum, 3 * HEAD_DIM // 2, 1)
        behind = pltpu.roll(key_sum, HEAD_DIM // 2, 1)
        turned = jnp.where(lanes < HEAD_DIM // 2, -ahead, behind)
        dk_refs[m][...] = (key_sum * cos_ref[m] - turned * sin_ref[m]).astype(BF16)
        dv_refs[m][...] = value_sum.astype(BF16)

    def clear(m):
        dk_refs[m][...] = jnp.zeros_like(dk_refs[m])
        dv_refs[m][...] = jnp.zeros_like(dv_refs[m])

    visit(0)
    for m in range(1, peers):
        pl.when((own ^ m) < own)(functools.partial(visit, m))
        pl.when((own ^ m) > own)(functools.partial(clear, m))
    for which in range(2):
        mine = slice(which * HEAD_DIM, (which + 1) * HEAD_DIM)
        for group in range(2):
            head = 2 * which + group
            dq_ref[head * HEAD_DIM : (head + 1) * HEAD_DIM, :] = (
                sum_ref[mine, group * rows : (group + 1) * rows] * SCALE
            )


def attend(own, queries, keys, values):
    width, rows = queries.shape
    kv_width = keys[0].shape[1]
    pairs = kv_width // (2 * HEAD_DIM)
    step = width // pairs
    heads = step // HEAD_DIM
    block = pl.BlockSpec((rows, 2 * HEAD_DIM), lambda p: (0, p))
    return pl.pallas_call(
        functools.partial(attend_kernel, len(keys)),
        grid=(pairs,),
        in_specs=[
            pl.BlockSpec(memory_space=pltpu.SMEM),
            pl.BlockSpec((step, rows), lambda p: (p, 0)),
            *([block] * (2 * len(keys))),
        ],
        out_specs=[
            pl.BlockSpec((step, rows), lambda p: (p, 0)),
            pl.BlockSpec((rows, step), lambda p: (0, p)),
            pl.BlockSpec((1, heads, rows), lambda p: (p, 0, 0)),
        ],
        out_shape=[
            jax.ShapeDtypeStruct((width, rows), F32),
            jax.ShapeDtypeStruct((rows, width), BF16),
            jax.ShapeDtypeStruct((pairs, heads, rows), F32),
        ],
        scratch_shapes=[
            pltpu.VMEM((2, 1, 2 * rows), F32),
            pltpu.VMEM((2, 1, 2 * rows), F32),
            pltpu.VMEM((2, HEAD_DIM, 2 * rows), F32),
        ],
        compiler_params=pltpu.CompilerParams(vmem_limit_bytes=48 * 1024 * 1024),
        cost_estimate=pl.CostEstimate(
            flops=2 * 2 * len(keys) * rows * rows * 4 * width,
            bytes_accessed=12 * rows * width,
            transcendentals=len(keys) * rows * rows * width // HEAD_DIM,
        ),
        name="attend",
    )(own, queries, *keys, *values)


def attend_back(own, queries, keys, values, grads, wide, logs, cosine, sine):
    width, rows = queries.shape
    kv_width = keys[0].shape[1]
    pairs = kv_width // (2 * HEAD_DIM)
    step = width // pairs
    heads = step // HEAD_DIM
    columns = pl.BlockSpec((step, rows), lambda p: (p, 0))
    table = pl.BlockSpec(cosine.shape, lambda p: (0, 0, 0))
    block = pl.BlockSpec((rows, 2 * HEAD_DIM), lambda p: (0, p))
    peers = len(keys)
    result = pl.pallas_call(
        functools.partial(attend_back_kernel, peers),
        grid=(pairs,),
        in_specs=[
            pl.BlockSpec(memory_space=pltpu.SMEM),
            columns,
            columns,
            columns,
            pl.BlockSpec((1, heads, rows), lambda p: (p, 0, 0)),
            table,
            table,
            *([block] * (2 * peers)),
        ],
        out_specs=[columns, *([block] * (2 * peers))],
        out_shape=[
            jax.ShapeDtypeStruct((width, rows), F32),
            *([jax.ShapeDtypeStruct((rows, kv_width), BF16)] * (2 * peers)),
        ],
        scratch_shapes=[pltpu.VMEM((2 * HEAD_DIM, 2 * rows), F32)],
        compiler_params=pltpu.CompilerParams(vmem_limit_bytes=48 * 1024 * 1024),
        cost_estimate=pl.CostEstimate(
            flops=5 * 2 * len(keys) * rows * rows * 4 * width,
            bytes_accessed=12 * rows * width,
            transcendentals=len(keys) * rows * rows * width // HEAD_DIM,
        ),
        name="attend_back",
    )(own, queries, grads, wide, logs, cosine, sine, *keys, *values)
    return result[0], result[1 : 1 + peers], result[1 + peers :]


def one_hot_rows(rank_row, rows):
    slots = lax.broadcasted_iota(jnp.int32, (rows, rank_row.shape[1]), 0)
    return slots == rank_row


def places(rank_ref, block, owned):
    return jnp.concatenate(
        [
            one_hot_rows(rank_ref[block, e : e + 1, :], CAP).astype(F32).astype(BF16)
            for e in range(owned)
        ],
        axis=0,
    )


def gather_rows(block, place, x, c, rank_ref, mask_ref, router_ref, rows_x, rows_c, rows_w):
    owned = rows_x.shape[0]
    at = slice(block * CAP, (block + 1) * CAP)
    select = places(rank_ref, place, owned)
    picked = mm(select, x).astype(BF16)
    upstream = mm(select, c).astype(BF16)
    logits = mm(picked, router_ref[...])
    named = mm(select, mask_ref[place], NT) > 0.5
    masked = jnp.where(named, logits, NEG)
    grown = jnp.where(named, jnp.exp(masked - jnp.max(masked, axis=1, keepdims=True)), 0.0)
    mass = jnp.sum(grown, axis=1, keepdims=True)
    weights = grown / jnp.where(mass > 0.0, mass, 1.0)
    for e in range(owned):
        part = slice(e * CAP, (e + 1) * CAP)
        rows_x[e, at, :] = picked[part]
        rows_c[e, at, :] = upstream[part]
        rows_w[e, at, :] = weights[part, e : e + 1]


def scatter_rows(block, select, rows):
    at = slice(block * CAP, (block + 1) * CAP)
    return mm(
        select, jnp.concatenate([rows[e, at, :] for e in range(rows.shape[0])], axis=0), TN
    ).astype(BF16)


def front_kernel(blocks, start, owned, near, here_ref, *refs):
    x_refs, refs = refs[:blocks], refs[blocks:]
    c_refs, refs = refs[:blocks], refs[blocks:]
    rank_ref, mask_ref, router_ref, wide_ref, down_ref = refs[:5]
    dx_refs, refs = refs[5 : 5 + blocks], refs[5 + blocks :]
    out_x, out_c, out_back, out_hidden, rows_x, rows_c, rows_w, chosen_ref = refs
    step = pl.program_id(0)
    tokens = x_refs[0].shape[0]
    size = down_ref.shape[1]

    def place(block):
        return block if near else here_ref[0] ^ (start + block)

    @pl.when(step == 0)
    def enter():
        for block in range(blocks):
            gather_rows(
                block,
                place(block),
                x_refs[block][...],
                c_refs[block][...] if near else c_refs[block][0],
                rank_ref,
                mask_ref,
                router_ref,
                rows_x,
                rows_c,
                rows_w,
            )

    e = step
    x = rows_x[e]
    c = rows_c[e]
    weight = rows_w[e]
    out_x[0] = x
    out_c[0] = c
    both = mm(x, wide_ref[0])
    gate, up = both[:, :size], both[:, size:]
    back = mm(c, down_ref[0], NT)
    sigmoid = 1.0 / (1.0 + jnp.exp(-gate))
    activated = gate * sigmoid
    hidden = activated * up
    scored = jnp.sum(hidden * back, axis=1, keepdims=True)
    for block in range(blocks):
        part = scored[block * CAP : (block + 1) * CAP]
        chosen_ref[e, block : block + 1, :] = jnp.sum(
            jnp.where(one_hot_rows(rank_ref[place(block), pl.ds(e, 1), :], CAP), part, 0.0),
            axis=0,
            keepdims=True,
        )
    out_hidden[0] = (hidden * weight).astype(BF16)
    back = back * weight
    gate_back = (back * up * sigmoid * (1.0 + gate * (1.0 - sigmoid))).astype(BF16)
    up_back = (back * activated).astype(BF16)
    backs = jnp.concatenate([gate_back, up_back], axis=1)
    out_back[0] = backs
    rows_x[e] = mm(backs, wide_ref[0], NT).astype(BF16)

    @pl.when(step == owned - 1)
    def leave():
        for block in range(blocks):
            select = places(rank_ref, place(block), owned)
            dx_refs[block][:tokens, :] = scatter_rows(block, select, rows_x)
            experts = mask_ref.shape[1]
            lines = lax.broadcasted_iota(jnp.int32, (experts, tokens), 0) - here_ref[0] * owned
            high, low = 0.0, 0.0
            for expert in range(owned):
                value = chosen_ref[expert, block : block + 1, :]
                rounded = value.astype(BF16).astype(F32)
                high = high + jnp.where(lines == expert, rounded, 0.0)
                low = low + jnp.where(lines == expert, value - rounded, 0.0)
            dx_refs[block][tokens:, :tokens] = high.astype(BF16)
            dx_refs[block][tokens:, tokens : 2 * tokens] = low.astype(BF16)


def rear_kernel(blocks, start, owned, near, first, here_ref, *refs):
    x_ref, c_ref, back_ref, hidden_ref, rank_ref, down_ref = refs[:6]
    old_ref = None if first else refs[6]
    refs = refs[6:] if first else refs[7:]
    y_refs, refs = refs[:blocks], refs[blocks:]
    grad_ref, rows_y = refs
    step = pl.program_id(0)
    width = x_ref.shape[2]

    def place(block):
        return block if near else here_ref[0] ^ (start + block)

    hidden = hidden_ref[0]
    for lines, left, right in (
        (slice(0, width), x_ref[0], back_ref[0]),
        (slice(width, grad_ref.shape[1]), hidden, c_ref[0]),
    ):
        grad = mm(left, right, TN)
        if old_ref is not None:
            grad = grad + old_ref[0, lines, :].astype(F32)
        grad_ref[0, lines, :] = grad.astype(BF16)
    rows_y[step] = mm(hidden, down_ref[0]).astype(BF16)

    @pl.when(step == owned - 1)
    def leave():
        for block in range(blocks):
            y_refs[block][...] = scatter_rows(
                block, places(rank_ref, place(block), owned), rows_y
            )


def run_front(here, start, x, c, rank, mask, router, w_wide, w_down):
    blocks = len(x)
    tokens, width = x[0].shape
    owned, hidden, _ = w_down.shape
    near = isinstance(c, list)
    once = pl.Buffered(1)
    rows = blocks * CAP
    long = tokens + mask.shape[1]

    def fixed(*shape):
        return pl.BlockSpec(shape, lambda s, h: (0,) * len(shape), pipeline_mode=once)

    def block_of(m):
        return pl.BlockSpec(
            (1, tokens, width), lambda s, h: (h[0] ^ m, 0, 0), pipeline_mode=once
        )

    def expert(*shape):
        return pl.BlockSpec((1, *shape), lambda s, h: (s, 0, 0))

    def shape(*dims):
        return jax.ShapeDtypeStruct(dims, BF16)

    params = pltpu.CompilerParams(vmem_limit_bytes=60 * 1024 * 1024)
    one = fixed(tokens, width)
    result = pl.pallas_call(
        functools.partial(front_kernel, blocks, start, owned, near),
        grid_spec=pltpu.PrefetchScalarGridSpec(
            num_scalar_prefetch=1,
            grid=(owned,),
            in_specs=[
                *([one] * blocks),
                *([one] * blocks if near else [block_of(start + i) for i in range(blocks)]),
                fixed(*rank.shape),
                fixed(*mask.shape),
                fixed(*router.shape),
                expert(width, 2 * hidden),
                expert(hidden, width),
            ],
            out_specs=[
                *([fixed(long, width)] * blocks),
                expert(rows, width),
                expert(rows, width),
                expert(rows, 2 * hidden),
                expert(rows, hidden),
            ],
            scratch_shapes=[
                pltpu.VMEM((owned, rows, width), BF16),
                pltpu.VMEM((owned, rows, width), BF16),
                pltpu.VMEM((owned, rows, 1), F32),
                pltpu.VMEM((owned, blocks, tokens), F32),
            ],
        ),
        out_shape=[
            *([shape(long, width)] * blocks),
            shape(owned, rows, width),
            shape(owned, rows, width),
            shape(owned, rows, 2 * hidden),
            shape(owned, rows, hidden),
        ],
        compiler_params=params,
        cost_estimate=pl.CostEstimate(
            flops=2 * owned * rows * width * (5 * hidden + 3 * tokens),
            bytes_accessed=8 * owned * rows * width,
            transcendentals=owned * rows * hidden,
        ),
        name="experts_front",
    )(here, *x, *(c if near else [c] * blocks), rank, mask, router, w_wide, w_down)
    return result[:blocks], result[blocks:]


def run_rear(here, start, blocks, near, kept, rank, w_down, old):
    owned, hidden, width = w_down.shape
    tokens = rank.shape[2]
    rows = blocks * CAP
    first = old is None

    def fixed(*shape):
        return pl.BlockSpec(
            shape, lambda s, h: (0,) * len(shape), pipeline_mode=pl.Buffered(1)
        )

    def expert(*shape):
        return pl.BlockSpec((1, *shape), lambda s, h: (s, 0, 0))

    def shape(*dims):
        return jax.ShapeDtypeStruct(dims, BF16)

    grad_shape = (owned, width + hidden, width)
    *y, grad = pl.pallas_call(
        functools.partial(rear_kernel, blocks, start, owned, near, first),
        grid_spec=pltpu.PrefetchScalarGridSpec(
            num_scalar_prefetch=1,
            grid=(owned,),
            in_specs=[
                expert(rows, width),
                expert(rows, width),
                expert(rows, 2 * hidden),
                expert(rows, hidden),
                fixed(*rank.shape),
                expert(hidden, width),
                *([] if first else [expert(*grad_shape[1:])]),
            ],
            out_specs=[*([fixed(tokens, width)] * blocks), expert(*grad_shape[1:])],
            scratch_shapes=[pltpu.VMEM((owned, rows, width), BF16)],
        ),
        out_shape=[*([shape(tokens, width)] * blocks), shape(*grad_shape)],
        compiler_params=pltpu.CompilerParams(vmem_limit_bytes=60 * 1024 * 1024),
        cost_estimate=pl.CostEstimate(
            flops=2 * owned * rows * width * (4 * hidden + tokens),
            bytes_accessed=8 * owned * rows * width,
            transcendentals=0,
        ),
        name="experts_rear",
    )(here, *kept, rank, w_down, *([] if first else [old]))
    return y, grad


def swap(value, axis, bit):
    peers = lax.axis_size(axis)
    return lax.ppermute(value, axis, [(i, i ^ bit) for i in range(peers)])


def add_low(left, right):
    return (left.astype(F32) + right.astype(F32)).astype(BF16)


def gather_blocks(value, axis, bits):
    held = {0: value}
    for bit in bits:
        for m in list(held):
            held[m | bit] = swap(held[m], axis, bit)
    return [held[m] for m in range(len(held))]


def reduce_step(held, axis, bit):
    if not isinstance(held, dict):
        held = dict(enumerate(held))
    else:
        held = dict(held)
    for m in sorted(held, reverse=True):
        if m & bit:
            arrived = swap(held.pop(m), axis, bit)
            held[m ^ bit] = add_low(held[m ^ bit], arrived)
    return held


def reduce_blocks(held, axis, bits):
    for bit in bits:
        held = reduce_step(held, axis, bit)
    return held[0]


def bits_of(axis):
    peers = lax.axis_size(axis)
    return [1 << i for i in range(peers.bit_length() - 1)]


def side_of(axis, bit):
    return (lax.axis_index(axis) // bit) % 2


def begin_sum(grad):
    rows = grad.shape[1]
    half = rows // 4
    rails = []
    for rail, (first, second) in enumerate(((1, 2), (2, 1))):
        base = rail * (rows // 2)
        one = side_of("ctx", first)
        other = lax.dynamic_slice_in_dim(grad, base + (1 - one) * half, half, 1)
        mine = lax.dynamic_slice_in_dim(grad, base + one * half, half, 1)
        rails.append(add_low(mine, swap(other, "ctx", first)))
    return rails


def middle_sum(rails):
    held = []
    for mine, (first, second) in zip(rails, ((1, 2), (2, 1))):
        two = side_of("ctx", second)
        quarter = mine.shape[1] // 2
        other = lax.dynamic_slice_in_dim(mine, (1 - two) * quarter, quarter, 1)
        mine = lax.dynamic_slice_in_dim(mine, two * quarter, quarter, 1)
        held.append(add_low(mine, swap(other, "ctx", second)))
    return held


def end_sum(grad, held):
    rows = grad.shape[1]
    half, quarter = rows // 4, rows // 8
    result = grad
    for rail, (mine, (first, second)) in enumerate(zip(held, ((1, 2), (2, 1)))):
        base = rail * (rows // 2)
        one, two = side_of("ctx", first), side_of("ctx", second)
        across = swap(mine, "ctx", second)
        pieces = (
            (mine, one, two),
            (across, one, 1 - two),
            (swap(mine, "ctx", first), 1 - one, two),
            (swap(across, "ctx", first), 1 - one, 1 - two),
        )
        for piece, row, column in pieces:
            result = lax.dynamic_update_slice_in_dim(
                result, piece, base + row * half + column * quarter, 1
            )
    return result


def after(values, *others):
    return lax.optimization_barrier((values, others))[0]


def per_device(
    tokens,
    attn_gain,
    query_weight,
    key_weight,
    value_weight,
    output_weight,
    moe_gain,
    w_router,
    routes,
    w_gate,
    w_up,
    w_down,
    cotangent,
):
    tok_rows, model_width = tokens.shape[1:]
    experts = w_router.shape[1]
    owned = w_gate.shape[0]
    peers = lax.axis_size("exp")
    here = lax.axis_index("exp")
    own = lax.axis_index("ctx")
    exp_bits = bits_of("exp")
    ctx_bits = bits_of("ctx")
    positions = own * tok_rows + jnp.arange(tok_rows, dtype=jnp.int32)
    half = HEAD_DIM // 2
    inverse = THETA ** (-jnp.arange(half, dtype=F32) * 2.0 / HEAD_DIM)
    angles = inverse[:, None] * positions.astype(F32)[None, :]
    cosine, sine = jnp.cos(angles), jnp.sin(angles)

    layer_inputs = tokens[0].astype(F32)
    scaled_one, factor_one = normalize(layer_inputs)
    first_normalized = (scaled_one * attn_gain).astype(BF16)
    value_rows = mm(first_normalized, value_weight).astype(BF16)
    key_rows = (
        rotate_columns(
            jnp.einsum("de,td->et", key_weight, first_normalized, preferred_element_type=F32),
            cosine,
            sine,
            1.0,
        )
        .astype(BF16)
        .T
    )
    peer_at = jnp.arange(lax.axis_size("ctx"), dtype=jnp.int32) ^ own
    lane_angles = (
        (peer_at[:, None] * tok_rows + jnp.arange(tok_rows, dtype=jnp.int32)).astype(F32)[..., None]
        * inverse
    )
    lane_cosine = jnp.tile(jnp.cos(lane_angles), (1, 1, 4))
    lane_sine = jnp.tile(jnp.sin(lane_angles), (1, 1, 4))
    keys = gather_blocks(key_rows, "ctx", ctx_bits)
    values = gather_blocks(value_rows, "ctx", ctx_bits[::-1])
    routes_here = routes[0].T.astype(BF16)
    spare = jnp.zeros((16 - routes_here.shape[0], tok_rows), BF16)
    packed = jnp.concatenate([routes_here, spare])
    packed = jnp.concatenate([packed, jnp.zeros((16, model_width - tok_rows), BF16)], axis=1)
    all_cot = lax.all_gather(jnp.concatenate([cotangent[0], packed]), "exp", axis=0)
    all_routes = all_cot[:, tok_rows : tok_rows + routes_here.shape[0], :tok_rows]
    near_routes = jnp.stack([routes_here, swap(routes_here, "exp", 1)])
    near_cot = [cotangent[0], swap(cotangent[0], "exp", 1)]
    queries = (
        rotate_columns(
            jnp.einsum("de,td->et", query_weight, first_normalized, preferred_element_type=F32),
            cosine,
            sine,
            1.0,
        ).astype(BF16)
        * SCALE
    ).astype(BF16)
    own_index = jnp.full((1,), own, jnp.int32)
    queries, lane_cosine, lane_sine = lax.optimization_barrier((queries, lane_cosine, lane_sine))
    attended_wide, attended_low, logs = attend(own_index, queries, keys, values)
    normed_blocks = gather_blocks(after(first_normalized, keys[-1], values[-1]), "ctx", ctx_bits)
    residual_stream = layer_inputs + mm(attended_low, output_weight)
    scaled_two, factor_two = normalize(residual_stream)
    normed_two = (scaled_two * moe_gain).astype(BF16)

    order = jnp.arange(experts, dtype=jnp.int32)
    order = ((order // owned) ^ here) * owned + order % owned
    permutation = (jnp.arange(experts, dtype=jnp.int32)[:, None] == order[None, :]).astype(BF16)
    upto = jnp.triu(jnp.ones((tok_rows, tok_rows), BF16))

    def find(block_routes):
        named = jnp.any(
            block_routes.astype(jnp.int32)[:, :, None, :] == order[:, None], axis=1
        )
        mask = named.astype(BF16)
        rank = jnp.einsum("bes,st->bet", mask[:, :owned], upto, preferred_element_type=F32)
        return jnp.where(named[:, :owned], rank.astype(jnp.int32) - 1, -1), mask

    router = mm(w_router, permutation).astype(BF16)
    here_index = jnp.full((1,), here, jnp.int32)

    x_blocks = {0: normed_two}
    for bit in exp_bits[:0:-1]:
        x_blocks[bit] = swap(normed_two, "exp", bit)
    x_blocks[1] = swap(normed_two, "exp", 1)
    w_wide = jnp.concatenate([w_gate, w_up], axis=2)
    mixed, dx, pending, grads = [], [], [], [None]

    def finish_rear(behind):
        start, end, kept = pending.pop(0)
        y_part, grad = run_rear(
            here_index,
            start,
            end - start,
            start == 0,
            after(kept, behind),
            near_found[0] if start == 0 else found[0],
            w_down,
            grads[-1],
        )
        mixed.extend(y_part)
        grads.append(grad)

    near_found, found = find(near_routes), find(all_routes)
    ends = [2, 4] + list(range(8, peers + 1, 4))
    for start, end in zip([0] + ends, ends):
        if start == 2:
            for m in range(4, peers, 2):
                top = 1 << (m.bit_length() - 1)
                if m != top:
                    low = (m - top) & (top - m)
                    x_blocks[m] = swap(x_blocks[m - low], "exp", low)
            x_blocks[3] = swap(x_blocks[2], "exp", 1)
        elif start == 4:
            for m in range(5, peers, 2):
                x_blocks[m] = swap(x_blocks[m - 1], "exp", 1)
        near = start == 0
        dx_part, kept = run_front(
            here_index,
            start,
            [x_blocks[m] for m in range(start, end)],
            near_cot if near else all_cot,
            *(near_found if near else found),
            router,
            w_wide,
            w_down,
        )
        dx += dx_part
        pending.append((start, end, kept))
        if near:
            finish_rear(dx_part)
        if end in (2, 4):
            waiting = [m for m in x_blocks if m >= end]
            behind = mixed[0] if near else dx_part[0]
            x_blocks.update(zip(waiting, after([x_blocks[m] for m in waiting], behind)))
    held = reduce_step(dx, "exp", exp_bits[0])
    for index, bit in enumerate(exp_bits[1:]):
        moved = [m for m in sorted(held, reverse=True) if m & bit]
        arrived = [swap(held[m], "exp", bit) for m in moved]
        for _ in range(-(-len(pending) // (len(exp_bits) - 1 - index))):
            finish_rear(list(held.values()))
        arrived = after(arrived, grads[-1])
        for m, part in zip(moved, arrived):
            held[m ^ bit] = add_low(held[m ^ bit], part)
            del held[m]
    dx_sum = held[0].astype(F32)
    old = grads[-1]

    rails = begin_sum(old)
    gate_grad = dx_sum[tok_rows:, :tok_rows] + dx_sum[tok_rows:, tok_rows : 2 * tok_rows]
    named_here = jnp.any(routes[0].T[:, None, :] == jnp.arange(experts)[:, None], axis=0)
    logits = jnp.einsum("de,td->et", w_router, normed_two, preferred_element_type=F32)
    masked = jnp.where(named_here, logits, NEG)
    grown = jnp.where(named_here, jnp.exp(masked - jnp.max(masked, axis=0, keepdims=True)), 0.0)
    gate_weights = grown / jnp.sum(grown, axis=0, keepdims=True)
    chosen_grad = gate_weights * (
        gate_grad - jnp.sum(gate_weights * gate_grad, axis=0, keepdims=True)
    )
    logit_grad = chosen_grad.astype(BF16)
    router_grad = jnp.einsum("td,et->ed", normed_two, logit_grad, preferred_element_type=F32)

    upstream = cotangent[0].astype(F32)
    normed_two_grad = mm(logit_grad, w_router.T, TN) + dx_sum[:tok_rows]
    gain_two_grad = jnp.sum(normed_two_grad * scaled_two, axis=0)
    residual_grad = upstream + norm_back(normed_two_grad * moe_gain, scaled_two, factor_two)
    residual_low = residual_grad.astype(BF16)
    attended_grad = mm(output_weight, residual_low, NT).astype(BF16)
    attended_grad, normed_blocks = lax.optimization_barrier((attended_grad, normed_blocks))
    wout_grad = mm(attended_low, residual_low, TN)
    query_grad, key_parts, value_parts = attend_back(
        own_index,
        queries,
        keys,
        values,
        attended_grad,
        attended_wide,
        logs,
        lane_cosine,
        lane_sine,
    )
    wk_grad = sum(mm(rows, part, TN) for rows, part in zip(normed_blocks, key_parts))
    wv_grad = sum(mm(rows, part, TN) for rows, part in zip(normed_blocks, value_parts))
    key_back = reduce_blocks(key_parts, "ctx", ctx_bits)
    value_back = reduce_blocks(value_parts, "ctx", ctx_bits[::-1])
    query_back = rotate_columns(query_grad, cosine, sine, -1.0).astype(BF16)
    wq_grad = jnp.einsum("td,et->de", first_normalized, query_back, preferred_element_type=F32)
    normed_one_grad = (
        jnp.einsum("et,de->td", query_back, query_weight, preferred_element_type=F32)
        + mm(key_back, key_weight, NT)
        + mm(value_back, value_weight, NT)
    )
    input_grad = residual_grad + norm_back(normed_one_grad * attn_gain, scaled_one, factor_one)
    spare = jnp.zeros((63 - experts, model_width), F32)
    small = jnp.concatenate([router_grad, gain_two_grad[None], spare])
    sums = tuple(part.astype(BF16) for part in (wout_grad, wq_grad, wk_grad, wv_grad, small))
    rails, sums = lax.optimization_barrier((rails, sums))
    sums = lax.psum(sums, ("ctx", "exp"))
    rails = middle_sum(rails)
    expert_grads = end_sum(old, after(rails, key_back, value_back))
    wide, hidden = w_gate.shape[1:]
    wgate_grad = expert_grads[:, :wide, :hidden].astype(F32)
    wup_grad = expert_grads[:, :wide, hidden:].astype(F32)
    down_grad = expert_grads[:, wide:].astype(F32)
    mixed = reduce_blocks(after(mixed, residual_low), "exp", exp_bits)
    output = (residual_stream + mixed.astype(F32)).astype(BF16)
    input_grad, output, wgate_grad, wup_grad, down_grad, sums = lax.optimization_barrier(
        (input_grad, output, wgate_grad, wup_grad, down_grad, sums)
    )
    wout_grad, wq_grad, wk_grad, wv_grad, small = (part.astype(F32) for part in sums)
    router_grad, gain_two_grad = small[:experts].T, small[experts]
    gain_one_grad = (
        jnp.sum(wq_grad * query_weight.astype(F32), axis=1)
        + jnp.sum(wk_grad * key_weight.astype(F32), axis=1)
        + jnp.sum(wv_grad * value_weight.astype(F32), axis=1)
    ) / attn_gain
    return (
        output[None],
        input_grad[None],
        gain_one_grad,
        wq_grad,
        wk_grad,
        wv_grad,
        wout_grad,
        gain_two_grad,
        router_grad,
        wgate_grad,
        wup_grad,
        down_grad,
    )


def solution(mesh):
    return jax.shard_map(
        per_device,
        mesh=mesh,
        in_specs=(
            P("exp", "ctx", None),
            P(),
            P(),
            P(),
            P(),
            P(),
            P(),
            P(),
            P("exp", "ctx", None),
            P("exp", None, None),
            P("exp", None, None),
            P("exp", None, None),
            P("exp", "ctx", None),
        ),
        out_specs=(
            P("exp", "ctx", None),
            P("exp", "ctx", None),
            P(),
            P(),
            P(),
            P(),
            P(),
            P(),
            P(),
            P("exp", None, None),
            P("exp", None, None),
            P("exp", None, None),
        ),
        check_vma=False,
    )
```

```python
import functools

import jax
import jax.numpy as jnp
from jax import lax
from jax.experimental import pallas as pl
from jax.experimental.pallas import tpu as pltpu
from jax.sharding import PartitionSpec as P

HEAD_DIM = 64
CAP = 192


SCALE = 0.015625
THETA = 10000.0
EPSILON = 1e-06
NEG = -1e30

F32 = jnp.float32
BF16 = jnp.bfloat16
NN = (((1,), (0,)), ((), ()))
NT = (((1,), (1,)), ((), ()))
TN = (((0,), (0,)), ((), ()))


def mm(left, right, dims=NN):
    return lax.dot_general(left, right, dims, preferred_element_type=F32)


def normalize(values):
    factor = lax.rsqrt(jnp.mean(values * values, axis=-1, keepdims=True) + EPSILON)
    return (values * factor, factor)


def norm_back(grad_scaled, scaled, factor):
    return factor * (grad_scaled - scaled * jnp.mean(grad_scaled * scaled, axis=-1, keepdims=True))


def rotate_columns(values, cosine, sine, direction):
    half = HEAD_DIM // 2
    split = values.reshape(-1, 2, half, values.shape[-1])
    first, second = split[:, 0], split[:, 1]
    turned = direction * sine
    return jnp.stack(
        [first * cosine - second * turned, second * cosine + first * turned], axis=1
    ).reshape(values.shape)


def head_columns(block, which):
    low = 2 * HEAD_DIM * which
    pair = jnp.concatenate(
        [block[low : low + HEAD_DIM], block[low + HEAD_DIM : low + 2 * HEAD_DIM]], axis=1
    )
    empty = jnp.zeros_like(pair)
    return jnp.concatenate([pair, empty] if which == 0 else [empty, pair], axis=0)


def causal(rows):
    keys = lax.broadcasted_iota(jnp.int32, (rows, rows), 0)
    places = lax.broadcasted_iota(jnp.int32, (rows, rows), 1)
    one = keys <= places
    return jnp.concatenate([one, one], axis=1)


def attend_kernel(peers, own_ref, q_ref, *refs):
    k_refs, v_refs = refs[:peers], refs[peers : 2 * peers]
    wide_ref, low_ref, log_ref, running_ref, mass_ref, total_ref = refs[2 * peers :]
    rows = q_ref.shape[1]
    own = own_ref[0]
    columns = [head_columns(q_ref[...], which) for which in range(2)]

    def visit(m):
        keys = k_refs[m][...]
        values = v_refs[m][...].T
        for which in range(2):
            scores = mm(keys, columns[which])
            if m == 0:
                scores = jnp.where(causal(rows), scores, NEG)
            newest = jnp.max(scores, axis=0, keepdims=True)
            if m > 0:
                newest = jnp.maximum(running_ref[which], newest)
            weights = jnp.exp(scores - newest)
            mass = jnp.sum(weights, axis=0, keepdims=True)
            mine = values[which * HEAD_DIM : (which + 1) * HEAD_DIM]
            total = mm(mine, weights.astype(BF16))
            if m > 0:
                rescale = jnp.exp(running_ref[which] - newest)
                mass = mass + mass_ref[which] * rescale
                total = total + total_ref[which] * rescale
            running_ref[which] = newest
            mass_ref[which] = mass
            total_ref[which] = total

    visit(0)
    for m in range(1, peers):
        pl.when((own ^ m) < own)(functools.partial(visit, m))
    for which in range(2):
        result = total_ref[which] / mass_ref[which]
        logs = running_ref[which] + jnp.log(mass_ref[which])
        for group in range(2):
            head = 2 * which + group
            part = slice(group * rows, (group + 1) * rows)
            wide_ref[head * HEAD_DIM : (head + 1) * HEAD_DIM, :] = result[:, part]
            log_ref[0, head : head + 1, :] = logs[:, part]
    low_ref[...] = wide_ref[...].T.astype(BF16)


def attend_back_kernel(peers, own_ref, q_ref, grad_ref, wide_ref, log_ref, cos_ref, sin_ref, *refs):
    k_refs, v_refs = refs[:peers], refs[peers : 2 * peers]
    dq_ref = refs[2 * peers]
    dk_refs = refs[2 * peers + 1 : 3 * peers + 1]
    dv_refs = refs[3 * peers + 1 : 4 * peers + 1]
    sum_ref = refs[4 * peers + 1]
    rows = q_ref.shape[1]
    own = own_ref[0]
    columns = [head_columns(q_ref[...], which) for which in range(2)]
    grads = [head_columns(grad_ref[...], which) for which in range(2)]
    offsets, logs = [], []
    for which in range(2):
        pieces = []
        for group in range(2):
            part = slice((2 * which + group) * HEAD_DIM, (2 * which + group + 1) * HEAD_DIM)
            pieces.append(
                jnp.sum(grad_ref[part, :].astype(F32) * wide_ref[part, :], axis=0, keepdims=True)
            )
        offsets.append(jnp.concatenate(pieces, axis=1))
        low = 2 * which
        logs.append(
            jnp.concatenate([log_ref[0, low : low + 1, :], log_ref[0, low + 1 : low + 2, :]], axis=1)
        )

    def visit(m):
        keys = k_refs[m][...]
        values = v_refs[m][...]
        turned = keys.T
        key_sum, value_sum = None, None
        for which in range(2):
            soft = jnp.exp(mm(keys, columns[which]) - logs[which])
            if m == 0:
                soft = jnp.where(causal(rows), soft, 0.0)
            prob_grad = mm(values, grads[which])
            score_grad = (soft * (prob_grad - offsets[which])).astype(BF16)
            value_part = mm(soft.astype(BF16), grads[which], NT)
            key_part = mm(score_grad, columns[which], NT)
            key_sum = key_part if key_sum is None else key_sum + key_part
            value_sum = value_part if value_sum is None else value_sum + value_part
            mine = slice(which * HEAD_DIM, (which + 1) * HEAD_DIM)
            part = mm(turned[mine], score_grad)
            sum_ref[mine, :] = part if m == 0 else sum_ref[mine, :] + part
        lanes = lax.broadcasted_iota(jnp.int32, key_sum.shape, 1) % HEAD_DIM
        ahead = pltpu.roll(key_sum, 3 * HEAD_DIM // 2, 1)
        behind = pltpu.roll(key_sum, HEAD_DIM // 2, 1)
        turned = jnp.where(lanes < HEAD_DIM // 2, -ahead, behind)
        dk_refs[m][...] = (key_sum * cos_ref[m] - turned * sin_ref[m]).astype(BF16)
        dv_refs[m][...] = value_sum.astype(BF16)

    def clear(m):
        dk_refs[m][...] = jnp.zeros_like(dk_refs[m])
        dv_refs[m][...] = jnp.zeros_like(dv_refs[m])

    visit(0)
    for m in range(1, peers):
        pl.when((own ^ m) < own)(functools.partial(visit, m))
        pl.when((own ^ m) > own)(functools.partial(clear, m))
    for which in range(2):
        mine = slice(which * HEAD_DIM, (which + 1) * HEAD_DIM)
        for group in range(2):
            head = 2 * which + group
            dq_ref[head * HEAD_DIM : (head + 1) * HEAD_DIM, :] = (
                sum_ref[mine, group * rows : (group + 1) * rows] * SCALE
            )


def attend(own, queries, keys, values):
    width, rows = queries.shape
    kv_width = keys[0].shape[1]
    pairs = kv_width // (2 * HEAD_DIM)
    step = width // pairs
    heads = step // HEAD_DIM
    block = pl.BlockSpec((rows, 2 * HEAD_DIM), lambda p: (0, p))
    return pl.pallas_call(
        functools.partial(attend_kernel, len(keys)),
        grid=(pairs,),
        in_specs=[
            pl.BlockSpec(memory_space=pltpu.SMEM),
            pl.BlockSpec((step, rows), lambda p: (p, 0)),
            *([block] * (2 * len(keys))),
        ],
        out_specs=[
            pl.BlockSpec((step, rows), lambda p: (p, 0)),
            pl.BlockSpec((rows, step), lambda p: (0, p)),
            pl.BlockSpec((1, heads, rows), lambda p: (p, 0, 0)),
        ],
        out_shape=[
            jax.ShapeDtypeStruct((width, rows), F32),
            jax.ShapeDtypeStruct((rows, width), BF16),
            jax.ShapeDtypeStruct((pairs, heads, rows), F32),
        ],
        scratch_shapes=[
            pltpu.VMEM((2, 1, 2 * rows), F32),
            pltpu.VMEM((2, 1, 2 * rows), F32),
            pltpu.VMEM((2, HEAD_DIM, 2 * rows), F32),
        ],
        compiler_params=pltpu.CompilerParams(vmem_limit_bytes=48 * 1024 * 1024),
        cost_estimate=pl.CostEstimate(
            flops=2 * 2 * len(keys) * rows * rows * 4 * width,
            bytes_accessed=12 * rows * width,
            transcendentals=len(keys) * rows * rows * width // HEAD_DIM,
        ),
        name="attend",
    )(own, queries, *keys, *values)


def attend_back(own, queries, keys, values, grads, wide, logs, cosine, sine):
    width, rows = queries.shape
    kv_width = keys[0].shape[1]
    pairs = kv_width // (2 * HEAD_DIM)
    step = width // pairs
    heads = step // HEAD_DIM
    columns = pl.BlockSpec((step, rows), lambda p: (p, 0))
    table = pl.BlockSpec(cosine.shape, lambda p: (0, 0, 0))
    block = pl.BlockSpec((rows, 2 * HEAD_DIM), lambda p: (0, p))
    peers = len(keys)
    result = pl.pallas_call(
        functools.partial(attend_back_kernel, peers),
        grid=(pairs,),
        in_specs=[
            pl.BlockSpec(memory_space=pltpu.SMEM),
            columns,
            columns,
            columns,
            pl.BlockSpec((1, heads, rows), lambda p: (p, 0, 0)),
            table,
            table,
            *([block] * (2 * peers)),
        ],
        out_specs=[columns, *([block] * (2 * peers))],
        out_shape=[
            jax.ShapeDtypeStruct((width, rows), F32),
            *([jax.ShapeDtypeStruct((rows, kv_width), BF16)] * (2 * peers)),
        ],
        scratch_shapes=[pltpu.VMEM((2 * HEAD_DIM, 2 * rows), F32)],
        compiler_params=pltpu.CompilerParams(vmem_limit_bytes=48 * 1024 * 1024),
        cost_estimate=pl.CostEstimate(
            flops=5 * 2 * len(keys) * rows * rows * 4 * width,
            bytes_accessed=12 * rows * width,
            transcendentals=len(keys) * rows * rows * width // HEAD_DIM,
        ),
        name="attend_back",
    )(own, queries, grads, wide, logs, cosine, sine, *keys, *values)
    return result[0], result[1 : 1 + peers], result[1 + peers :]


def one_hot_rows(rank_row, rows):
    slots = lax.broadcasted_iota(jnp.int32, (rows, rank_row.shape[1]), 0)
    return slots == rank_row


def places(rank_ref, block, owned):
    return jnp.concatenate(
        [
            one_hot_rows(rank_ref[block, e : e + 1, :], CAP).astype(F32).astype(BF16)
            for e in range(owned)
        ],
        axis=0,
    )


def gather_rows(block, place, x, c, rank_ref, mask_ref, router_ref, rows_x, rows_c, rows_w):
    owned = rows_x.shape[0]
    at = slice(block * CAP, (block + 1) * CAP)
    select = places(rank_ref, place, owned)
    picked = mm(select, x).astype(BF16)
    upstream = mm(select, c).astype(BF16)
    logits = mm(picked, router_ref[...])
    named = mm(select, mask_ref[place], NT) > 0.5
    masked = jnp.where(named, logits, NEG)
    grown = jnp.where(named, jnp.exp(masked - jnp.max(masked, axis=1, keepdims=True)), 0.0)
    mass = jnp.sum(grown, axis=1, keepdims=True)
    weights = grown / jnp.where(mass > 0.0, mass, 1.0)
    for e in range(owned):
        part = slice(e * CAP, (e + 1) * CAP)
        rows_x[e, at, :] = picked[part]
        rows_c[e, at, :] = upstream[part]
        rows_w[e, at, :] = weights[part, e : e + 1]


def scatter_rows(block, select, rows):
    at = slice(block * CAP, (block + 1) * CAP)
    return mm(
        select, jnp.concatenate([rows[e, at, :] for e in range(rows.shape[0])], axis=0), TN
    ).astype(BF16)


def front_kernel(blocks, start, owned, near, here_ref, *refs):
    x_refs, refs = refs[:blocks], refs[blocks:]
    c_refs, refs = refs[:blocks], refs[blocks:]
    rank_ref, mask_ref, router_ref, wide_ref, down_ref = refs[:5]
    dx_refs, refs = refs[5 : 5 + blocks], refs[5 + blocks :]
    out_x, out_c, out_back, out_hidden, rows_x, rows_c, rows_w, chosen_ref = refs
    step = pl.program_id(0)
    tokens = x_refs[0].shape[0]
    size = down_ref.shape[1]

    def place(block):
        return block if near else here_ref[0] ^ (start + block)

    @pl.when(step == 0)
    def enter():
        for block in range(blocks):
            gather_rows(
                block,
                place(block),
                x_refs[block][...],
                c_refs[block][...] if near else c_refs[block][0],
                rank_ref,
                mask_ref,
                router_ref,
                rows_x,
                rows_c,
                rows_w,
            )

    e = step
    x = rows_x[e]
    c = rows_c[e]
    weight = rows_w[e]
    out_x[0] = x
    out_c[0] = c
    both = mm(x, wide_ref[0])
    gate, up = both[:, :size], both[:, size:]
    back = mm(c, down_ref[0], NT)
    sigmoid = 1.0 / (1.0 + jnp.exp(-gate))
    activated = gate * sigmoid
    hidden = activated * up
    scored = jnp.sum(hidden * back, axis=1, keepdims=True)
    for block in range(blocks):
        part = scored[block * CAP : (block + 1) * CAP]
        chosen_ref[e, block : block + 1, :] = jnp.sum(
            jnp.where(one_hot_rows(rank_ref[place(block), pl.ds(e, 1), :], CAP), part, 0.0),
            axis=0,
            keepdims=True,
        )
    out_hidden[0] = (hidden * weight).astype(BF16)
    back = back * weight
    gate_back = (back * up * sigmoid * (1.0 + gate * (1.0 - sigmoid))).astype(BF16)
    up_back = (back * activated).astype(BF16)
    backs = jnp.concatenate([gate_back, up_back], axis=1)
    out_back[0] = backs
    rows_x[e] = mm(backs, wide_ref[0], NT).astype(BF16)

    @pl.when(step == owned - 1)
    def leave():
        for block in range(blocks):
            select = places(rank_ref, place(block), owned)
            dx_refs[block][:tokens, :] = scatter_rows(block, select, rows_x)
            experts = mask_ref.shape[1]
            lines = lax.broadcasted_iota(jnp.int32, (experts, tokens), 0) - here_ref[0] * owned
            high, low = 0.0, 0.0
            for expert in range(owned):
                value = chosen_ref[expert, block : block + 1, :]
                rounded = value.astype(BF16).astype(F32)
                high = high + jnp.where(lines == expert, rounded, 0.0)
                low = low + jnp.where(lines == expert, value - rounded, 0.0)
            dx_refs[block][tokens:, :tokens] = high.astype(BF16)
            dx_refs[block][tokens:, tokens : 2 * tokens] = low.astype(BF16)


def rear_kernel(blocks, start, owned, near, first, here_ref, *refs):
    x_ref, c_ref, back_ref, hidden_ref, rank_ref, down_ref = refs[:6]
    old_ref = None if first else refs[6]
    refs = refs[6:] if first else refs[7:]
    y_refs, refs = refs[:blocks], refs[blocks:]
    grad_ref, rows_y = refs
    step = pl.program_id(0)
    width = x_ref.shape[2]

    def place(block):
        return block if near else here_ref[0] ^ (start + block)

    hidden = hidden_ref[0]
    for lines, left, right in (
        (slice(0, width), x_ref[0], back_ref[0]),
        (slice(width, grad_ref.shape[1]), hidden, c_ref[0]),
    ):
        grad = mm(left, right, TN)
        if old_ref is not None:
            grad = grad + old_ref[0, lines, :].astype(F32)
        grad_ref[0, lines, :] = grad.astype(BF16)
    rows_y[step] = mm(hidden, down_ref[0]).astype(BF16)

    @pl.when(step == owned - 1)
    def leave():
        for block in range(blocks):
            y_refs[block][...] = scatter_rows(
                block, places(rank_ref, place(block), owned), rows_y
            )


def run_front(here, start, x, c, rank, mask, router, w_wide, w_down):
    blocks = len(x)
    tokens, width = x[0].shape
    owned, hidden, _ = w_down.shape
    near = isinstance(c, list)
    once = pl.Buffered(1)
    rows = blocks * CAP
    long = tokens + mask.shape[1]

    def fixed(*shape):
        return pl.BlockSpec(shape, lambda s, h: (0,) * len(shape), pipeline_mode=once)

    def block_of(m):
        return pl.BlockSpec(
            (1, tokens, width), lambda s, h: (h[0] ^ m, 0, 0), pipeline_mode=once
        )

    def expert(*shape):
        return pl.BlockSpec((1, *shape), lambda s, h: (s, 0, 0))

    def shape(*dims):
        return jax.ShapeDtypeStruct(dims, BF16)

    params = pltpu.CompilerParams(vmem_limit_bytes=60 * 1024 * 1024)
    one = fixed(tokens, width)
    result = pl.pallas_call(
        functools.partial(front_kernel, blocks, start, owned, near),
        grid_spec=pltpu.PrefetchScalarGridSpec(
            num_scalar_prefetch=1,
            grid=(owned,),
            in_specs=[
                *([one] * blocks),
                *([one] * blocks if near else [block_of(start + i) for i in range(blocks)]),
                fixed(*rank.shape),
                fixed(*mask.shape),
                fixed(*router.shape),
                expert(width, 2 * hidden),
                expert(hidden, width),
            ],
            out_specs=[
                *([fixed(long, width)] * blocks),
                expert(rows, width),
                expert(rows, width),
                expert(rows, 2 * hidden),
                expert(rows, hidden),
            ],
            scratch_shapes=[
                pltpu.VMEM((owned, rows, width), BF16),
                pltpu.VMEM((owned, rows, width), BF16),
                pltpu.VMEM((owned, rows, 1), F32),
                pltpu.VMEM((owned, blocks, tokens), F32),
            ],
        ),
        out_shape=[
            *([shape(long, width)] * blocks),
            shape(owned, rows, width),
            shape(owned, rows, width),
            shape(owned, rows, 2 * hidden),
            shape(owned, rows, hidden),
        ],
        compiler_params=params,
        cost_estimate=pl.CostEstimate(
            flops=2 * owned * rows * width * (5 * hidden + 3 * tokens),
            bytes_accessed=8 * owned * rows * width,
            transcendentals=owned * rows * hidden,
        ),
        name="experts_front",
    )(here, *x, *(c if near else [c] * blocks), rank, mask, router, w_wide, w_down)
    return result[:blocks], result[blocks:]


def run_rear(here, start, blocks, near, kept, rank, w_down, old):
    owned, hidden, width = w_down.shape
    tokens = rank.shape[2]
    rows = blocks * CAP
    first = old is None

    def fixed(*shape):
        return pl.BlockSpec(
            shape, lambda s, h: (0,) * len(shape), pipeline_mode=pl.Buffered(1)
        )

    def expert(*shape):
        return pl.BlockSpec((1, *shape), lambda s, h: (s, 0, 0))

    def shape(*dims):
        return jax.ShapeDtypeStruct(dims, BF16)

    grad_shape = (owned, width + hidden, width)
    *y, grad = pl.pallas_call(
        functools.partial(rear_kernel, blocks, start, owned, near, first),
        grid_spec=pltpu.PrefetchScalarGridSpec(
            num_scalar_prefetch=1,
            grid=(owned,),
            in_specs=[
                expert(rows, width),
                expert(rows, width),
                expert(rows, 2 * hidden),
                expert(rows, hidden),
                fixed(*rank.shape),
                expert(hidden, width),
                *([] if first else [expert(*grad_shape[1:])]),
            ],
            out_specs=[*([fixed(tokens, width)] * blocks), expert(*grad_shape[1:])],
            scratch_shapes=[pltpu.VMEM((owned, rows, width), BF16)],
        ),
        out_shape=[*([shape(tokens, width)] * blocks), shape(*grad_shape)],
        compiler_params=pltpu.CompilerParams(vmem_limit_bytes=60 * 1024 * 1024),
        cost_estimate=pl.CostEstimate(
            flops=2 * owned * rows * width * (4 * hidden + tokens),
            bytes_accessed=8 * owned * rows * width,
            transcendentals=0,
        ),
        name="experts_rear",
    )(here, *kept, rank, w_down, *([] if first else [old]))
    return y, grad


def swap(value, axis, bit):
    peers = lax.axis_size(axis)
    return lax.ppermute(value, axis, [(i, i ^ bit) for i in range(peers)])


def add_low(left, right):
    return (left.astype(F32) + right.astype(F32)).astype(BF16)


def gather_blocks(value, axis, bits):
    held = {0: value}
    for bit in bits:
        for m in list(held):
            held[m | bit] = swap(held[m], axis, bit)
    return [held[m] for m in range(len(held))]


def reduce_step(held, axis, bit):
    if not isinstance(held, dict):
        held = dict(enumerate(held))
    else:
        held = dict(held)
    for m in sorted(held, reverse=True):
        if m & bit:
            arrived = swap(held.pop(m), axis, bit)
            held[m ^ bit] = add_low(held[m ^ bit], arrived)
    return held


def reduce_blocks(held, axis, bits):
    for bit in bits:
        held = reduce_step(held, axis, bit)
    return held[0]


def bits_of(axis):
    peers = lax.axis_size(axis)
    return [1 << i for i in range(peers.bit_length() - 1)]


def side_of(axis, bit):
    return (lax.axis_index(axis) // bit) % 2


RAILS = ((1, 2), (2, 1))


def begin_sum(grad):
    columns = grad.shape[2]
    half = columns // 4
    rails = []
    for rail, (first, _) in enumerate(RAILS):
        base = rail * (columns // 2)
        one = side_of("ctx", first)
        other = lax.dynamic_slice_in_dim(grad, base + (1 - one) * half, half, 2)
        mine = lax.dynamic_slice_in_dim(grad, base + one * half, half, 2)
        rails.append(add_low(mine, swap(other, "ctx", first)))
    return rails


def middle_sum(rails):
    held = []
    for mine, (_, second) in zip(rails, RAILS):
        two = side_of("ctx", second)
        quarter = mine.shape[2] // 2
        other = lax.dynamic_slice_in_dim(mine, (1 - two) * quarter, quarter, 2)
        mine = lax.dynamic_slice_in_dim(mine, two * quarter, quarter, 2)
        held.append(add_low(mine, swap(other, "ctx", second)))
    return held


def end_sum(held, others):
    across = [swap(mine, "ctx", second) for mine, (_, second) in zip(held, RAILS)]
    along = [swap(mine, "ctx", first) for mine, (first, _) in zip(held, RAILS)]
    across, others = lax.optimization_barrier((across, others))
    pieces, spots = [], []
    for index, (first, second) in enumerate(RAILS):
        one, two = side_of("ctx", first), side_of("ctx", second)
        pieces += [held[index], across[index], along[index], swap(across[index], "ctx", first)]
        spots += [2 * one + two, 2 * one + 1 - two, 2 * (1 - one) + two, 2 * (1 - one) + 1 - two]
    return pieces, jnp.stack(spots).astype(jnp.int32), others


def assemble_kernel(width, spots_ref, *refs):
    pieces, (gate_ref, up_ref, down_ref) = refs[:8], refs[8:]
    part = pieces[0].shape[2]
    for index in range(8):
        out_ref = gate_ref if index < 4 else up_ref
        spot = spots_ref[index]
        out_ref[0, :, pl.ds(pl.multiple_of(spot * part, part), part)] = pieces[index][
            0, :width
        ].astype(F32)
        spot = spot + index // 4 * 4
        down_ref[0, :, pl.ds(pl.multiple_of(spot * part, part), part)] = pieces[index][
            0, width:
        ].astype(F32)


def assemble(pieces, spots, width):
    owned, rows, part = pieces[0].shape
    hidden = rows - width

    def block(*shape):
        return pl.BlockSpec((1, *shape), lambda e, at: (e, 0, 0))

    return pl.pallas_call(
        functools.partial(assemble_kernel, width),
        grid_spec=pltpu.PrefetchScalarGridSpec(
            num_scalar_prefetch=1,
            grid=(owned,),
            in_specs=[block(rows, part)] * 8,
            out_specs=[block(width, 4 * part), block(width, 4 * part), block(hidden, 8 * part)],
        ),
        out_shape=[
            jax.ShapeDtypeStruct((owned, width, 4 * part), F32),
            jax.ShapeDtypeStruct((owned, width, 4 * part), F32),
            jax.ShapeDtypeStruct((owned, hidden, 8 * part), F32),
        ],
        compiler_params=pltpu.CompilerParams(vmem_limit_bytes=48 * 1024 * 1024),
        name="assemble",
    )(spots, *pieces)


def after(values, *others):
    return lax.optimization_barrier((values, others))[0]


def per_device(
    tokens,
    attn_gain,
    query_weight,
    key_weight,
    value_weight,
    output_weight,
    moe_gain,
    w_router,
    routes,
    w_gate,
    w_up,
    w_down,
    cotangent,
):
    tok_rows, model_width = tokens.shape[1:]
    experts = w_router.shape[1]
    owned = w_gate.shape[0]
    peers = lax.axis_size("exp")
    here = lax.axis_index("exp")
    own = lax.axis_index("ctx")
    exp_bits = bits_of("exp")
    ctx_bits = bits_of("ctx")
    positions = own * tok_rows + jnp.arange(tok_rows, dtype=jnp.int32)
    half = HEAD_DIM // 2
    inverse = THETA ** (-jnp.arange(half, dtype=F32) * 2.0 / HEAD_DIM)
    angles = inverse[:, None] * positions.astype(F32)[None, :]
    cosine, sine = jnp.cos(angles), jnp.sin(angles)

    layer_inputs = tokens[0].astype(F32)
    scaled_one, factor_one = normalize(layer_inputs)
    first_normalized = (scaled_one * attn_gain).astype(BF16)
    value_rows = mm(first_normalized, value_weight).astype(BF16)
    key_rows = (
        rotate_columns(
            jnp.einsum("de,td->et", key_weight, first_normalized, preferred_element_type=F32),
            cosine,
            sine,
            1.0,
        )
        .astype(BF16)
        .T
    )
    peer_at = jnp.arange(lax.axis_size("ctx"), dtype=jnp.int32) ^ own
    lane_angles = (
        (peer_at[:, None] * tok_rows + jnp.arange(tok_rows, dtype=jnp.int32)).astype(F32)[..., None]
        * inverse
    )
    lane_cosine = jnp.tile(jnp.cos(lane_angles), (1, 1, 4))
    lane_sine = jnp.tile(jnp.sin(lane_angles), (1, 1, 4))
    keys = gather_blocks(key_rows, "ctx", ctx_bits)
    values = gather_blocks(value_rows, "ctx", ctx_bits[::-1])
    routes_here = routes[0].T.astype(BF16)
    spare = jnp.zeros((16 - routes_here.shape[0], tok_rows), BF16)
    packed = jnp.concatenate([routes_here, spare])
    packed = jnp.concatenate([packed, jnp.zeros((16, model_width - tok_rows), BF16)], axis=1)
    all_cot = lax.all_gather(jnp.concatenate([cotangent[0], packed]), "exp", axis=0)
    all_routes = all_cot[:, tok_rows : tok_rows + routes_here.shape[0], :tok_rows]
    near_routes = jnp.stack([routes_here, swap(routes_here, "exp", 1)])
    near_cot = [cotangent[0], swap(cotangent[0], "exp", 1)]
    queries = (
        rotate_columns(
            jnp.einsum("de,td->et", query_weight, first_normalized, preferred_element_type=F32),
            cosine,
            sine,
            1.0,
        ).astype(BF16)
        * SCALE
    ).astype(BF16)
    own_index = jnp.full((1,), own, jnp.int32)
    queries, lane_cosine, lane_sine = lax.optimization_barrier((queries, lane_cosine, lane_sine))
    attended_wide, attended_low, logs = attend(own_index, queries, keys, values)
    normed_blocks = gather_blocks(after(first_normalized, keys[-1], values[-1]), "ctx", ctx_bits)
    residual_stream = layer_inputs + mm(attended_low, output_weight)
    scaled_two, factor_two = normalize(residual_stream)
    normed_two = (scaled_two * moe_gain).astype(BF16)

    order = jnp.arange(experts, dtype=jnp.int32)
    order = ((order // owned) ^ here) * owned + order % owned
    permutation = (jnp.arange(experts, dtype=jnp.int32)[:, None] == order[None, :]).astype(BF16)
    upto = jnp.triu(jnp.ones((tok_rows, tok_rows), BF16))

    def find(block_routes):
        named = jnp.any(
            block_routes.astype(jnp.int32)[:, :, None, :] == order[:, None], axis=1
        )
        mask = named.astype(BF16)
        rank = jnp.einsum("bes,st->bet", mask[:, :owned], upto, preferred_element_type=F32)
        return jnp.where(named[:, :owned], rank.astype(jnp.int32) - 1, -1), mask

    router = mm(w_router, permutation).astype(BF16)
    here_index = jnp.full((1,), here, jnp.int32)

    x_blocks = {0: normed_two}
    for bit in exp_bits[:0:-1]:
        x_blocks[bit] = swap(normed_two, "exp", bit)
    x_blocks[1] = swap(normed_two, "exp", 1)
    w_wide = jnp.concatenate([w_gate, w_up], axis=2)
    mixed, dx, pending, grads = [], [], [], [None]

    def finish_rear(behind):
        start, end, kept = pending.pop(0)
        y_part, grad = run_rear(
            here_index,
            start,
            end - start,
            start == 0,
            after(kept, behind),
            near_found[0] if start == 0 else found[0],
            w_down,
            grads[-1],
        )
        mixed.extend(y_part)
        grads.append(grad)

    near_found, found = find(near_routes), find(all_routes)
    ends = [2, 4] + list(range(8, peers + 1, 4))
    for start, end in zip([0] + ends, ends):
        if start == 2:
            for m in range(4, peers, 2):
                top = 1 << (m.bit_length() - 1)
                if m != top:
                    low = (m - top) & (top - m)
                    x_blocks[m] = swap(x_blocks[m - low], "exp", low)
            x_blocks[3] = swap(x_blocks[2], "exp", 1)
        elif start == 4:
            for m in range(5, peers, 2):
                x_blocks[m] = swap(x_blocks[m - 1], "exp", 1)
        near = start == 0
        dx_part, kept = run_front(
            here_index,
            start,
            [x_blocks[m] for m in range(start, end)],
            near_cot if near else all_cot,
            *(near_found if near else found),
            router,
            w_wide,
            w_down,
        )
        dx += dx_part
        pending.append((start, end, kept))
        if near:
            finish_rear(dx_part)
        if end in (2, 4):
            waiting = [m for m in x_blocks if m >= end]
            behind = mixed[0] if near else dx_part[0]
            x_blocks.update(zip(waiting, after([x_blocks[m] for m in waiting], behind)))
    held = reduce_step(dx, "exp", exp_bits[0])
    for index, bit in enumerate(exp_bits[1:]):
        moved = [m for m in sorted(held, reverse=True) if m & bit]
        arrived = [swap(held[m], "exp", bit) for m in moved]
        for _ in range(-(-len(pending) // (len(exp_bits) - 1 - index))):
            finish_rear(list(held.values()))
        arrived = after(arrived, grads[-1])
        for m, part in zip(moved, arrived):
            held[m ^ bit] = add_low(held[m ^ bit], part)
            del held[m]
    dx_sum = held[0].astype(F32)
    old = grads[-1]

    rails = begin_sum(old)
    gate_grad = dx_sum[tok_rows:, :tok_rows] + dx_sum[tok_rows:, tok_rows : 2 * tok_rows]
    named_here = jnp.any(routes[0].T[:, None, :] == jnp.arange(experts)[:, None], axis=0)
    logits = jnp.einsum("de,td->et", w_router, normed_two, preferred_element_type=F32)
    masked = jnp.where(named_here, logits, NEG)
    grown = jnp.where(named_here, jnp.exp(masked - jnp.max(masked, axis=0, keepdims=True)), 0.0)
    gate_weights = grown / jnp.sum(grown, axis=0, keepdims=True)
    chosen_grad = gate_weights * (
        gate_grad - jnp.sum(gate_weights * gate_grad, axis=0, keepdims=True)
    )
    logit_grad = chosen_grad.astype(BF16)
    router_grad = jnp.einsum("td,et->ed", normed_two, logit_grad, preferred_element_type=F32)

    upstream = cotangent[0].astype(F32)
    normed_two_grad = mm(logit_grad, w_router.T, TN) + dx_sum[:tok_rows]
    gain_two_grad = jnp.sum(normed_two_grad * scaled_two, axis=0)
    residual_grad = upstream + norm_back(normed_two_grad * moe_gain, scaled_two, factor_two)
    residual_low = residual_grad.astype(BF16)
    attended_grad = mm(output_weight, residual_low, NT).astype(BF16)
    attended_grad, normed_blocks = lax.optimization_barrier((attended_grad, normed_blocks))
    wout_grad = mm(attended_low, residual_low, TN)
    query_grad, key_parts, value_parts = attend_back(
        own_index,
        queries,
        keys,
        values,
        attended_grad,
        attended_wide,
        logs,
        lane_cosine,
        lane_sine,
    )
    wk_grad = sum(mm(rows, part, TN) for rows, part in zip(normed_blocks, key_parts))
    wv_grad = sum(mm(rows, part, TN) for rows, part in zip(normed_blocks, value_parts))
    key_back = reduce_blocks(key_parts, "ctx", ctx_bits)
    value_back = reduce_blocks(value_parts, "ctx", ctx_bits[::-1])
    query_back = rotate_columns(query_grad, cosine, sine, -1.0).astype(BF16)
    wq_grad = jnp.einsum("td,et->de", first_normalized, query_back, preferred_element_type=F32)
    normed_one_grad = (
        jnp.einsum("et,de->td", query_back, query_weight, preferred_element_type=F32)
        + mm(key_back, key_weight, NT)
        + mm(value_back, value_weight, NT)
    )
    input_grad = residual_grad + norm_back(normed_one_grad * attn_gain, scaled_one, factor_one)
    spare = jnp.zeros((63 - experts, model_width), F32)
    small = jnp.concatenate([router_grad, gain_two_grad[None], spare])
    sums = tuple(part.astype(BF16) for part in (wout_grad, wq_grad, wk_grad, wv_grad, small))
    rails, sums = lax.optimization_barrier((rails, sums))
    sums = lax.psum(sums, ("ctx", "exp"))
    rails = middle_sum(rails)
    mixed = after(mixed, residual_low)
    for bit in exp_bits[:-1]:
        mixed = reduce_step(mixed, "exp", bit)
    arrived = swap(mixed[exp_bits[-1]], "exp", exp_bits[-1])
    pieces, spots, (sums, arrived) = end_sum(
        after(rails, key_back, value_back), (sums, arrived)
    )
    wgate_grad, wup_grad, down_grad = assemble(pieces, spots, w_gate.shape[1])
    mixed = add_low(mixed[0], arrived)
    output = (residual_stream + mixed.astype(F32)).astype(BF16)
    wout_grad, wq_grad, wk_grad, wv_grad, small = (part.astype(F32) for part in sums)
    router_grad, gain_two_grad = small[:experts].T, small[experts]
    gain_one_grad = (
        jnp.sum(wq_grad * query_weight.astype(F32), axis=1)
        + jnp.sum(wk_grad * key_weight.astype(F32), axis=1)
        + jnp.sum(wv_grad * value_weight.astype(F32), axis=1)
    ) / attn_gain
    return (
        output[None],
        input_grad[None],
        gain_one_grad,
        wq_grad,
        wk_grad,
        wv_grad,
        wout_grad,
        gain_two_grad,
        router_grad,
        wgate_grad,
        wup_grad,
        down_grad,
    )


def solution(mesh):
    return jax.shard_map(
        per_device,
        mesh=mesh,
        in_specs=(
            P("exp", "ctx", None),
            P(),
            P(),
            P(),
            P(),
            P(),
            P(),
            P(),
            P("exp", "ctx", None),
            P("exp", None, None),
            P("exp", None, None),
            P("exp", None, None),
            P("exp", "ctx", None),
        ),
        out_specs=(
            P("exp", "ctx", None),
            P("exp", "ctx", None),
            P(),
            P(),
            P(),
            P(),
            P(),
            P(),
            P(),
            P("exp", None, None),
            P("exp", None, None),
            P("exp", None, None),
        ),
        check_vma=False,
    )
```
